32 devices in a mesh: groups: 2 (over y), expert: 4 (over z), dp: 2 (over x), tensor: 2 (over core).
Axes of the slice: x: 2, y: 2, z: 4, core: 2. Of those that a mesh axis runs over, the one named last changes fastest.
Arguments:
- tokens: bfloat16 [2048, 2048], P(('groups', 'expert', 'dp'), 'tensor'), parts along dimension 0, may hold values from -6 to 6
- cotangent: bfloat16 [2048, 2048], P(('groups', 'expert', 'dp'), 'tensor'), parts along dimension 0, may hold values from -6 to 6
- expert_ids: int32 [2048, 2], P(('groups', 'expert', 'dp')), parts along dimension 0, may hold values from 0 to 3, all different within a row; in each aligned block of 128 rows (0 to 127, 128 to 255, ...) at most 96 rows name the same one
- gate_probs: float32 [2048, 2], P(('groups', 'expert', 'dp')), parts along dimension 0, may hold values from 0.05 to 1
- w_gate: bfloat16 [4, 2048, 1408], P('expert', 'dp', 'tensor'), may hold values from -0.125 to 0.125
- w_up: bfloat16 [4, 2048, 1408], P('expert', 'dp', 'tensor'), may hold values from -0.125 to 0.125
- w_down: bfloat16 [4, 1408, 2048], P('expert', 'dp', 'tensor'), may hold values from -0.15625 to 0.15625
Outputs:
- layer_out: bfloat16 [2048, 2048], P(('groups', 'expert', 'dp'), 'tensor'), parts along dimension 0
- grad_tokens: bfloat16 [2048, 2048], P(('groups', 'expert', 'dp'), 'tensor'), parts along dimension 0
- grad_probs: float32 [2048, 2], P(('groups', 'expert', 'dp')), parts along dimension 0
The draws below stay inside these ranges and needn't reach their ends.
There are 2 independent parts, one for each index of `groups`. The reference program is written for one: setup_inputs(seed, part) draws one part's arguments, and reference() takes and returns one part's arrays. A program takes and returns all parts, laid end to end along the dimension named above; an argument that names none is the same for every part. Nothing has to cross between parts.
Inputs may be any that keep to these rules, and one draw needn't show every extreme that they name: `expert_ids`: each token names 2 different experts. Among the 128 tokens of one index of expert and dp (aligned blocks of 128 rows), no expert is named more than 96 times, a bound that some block reaches.
All inputs are finite; a program needn't handle non-finite values.
Results may differ from the reference program's by a relative error of at most 0.015.
Values may be sent and summed in bfloat16 or wider, within the bound.
No kernel may reach another device: no remote copies, remote signals or barrier semaphores. Data moves between devices by JAX's collectives and lax.ppermute only.
A program may use at most 64 MiB of HBM per device.

```python
import math
import jax
import jax.numpy as jnp
import numpy as np
from jax import lax

D = 2048
FF = 1408
TOP = 2
TOK_DEV = 128
EXPERTS = 4
TOKENS = 1024
CAP = 96
N_EXPERT = 4
N_DP = 2
N_TENSOR = 2


def shard_levels(own_key, extent, cuts, smallest, high):
    def one(dim, shards_of):
        heights = jax.random.uniform(jax.random.fold_in(jax.random.fold_in(own_key, 6), dim), (shards_of,), jnp.float32, smallest / len(cuts), high / len(cuts))
        return jnp.repeat(jnp.exp(heights), extent[dim] // shards_of).reshape((-1,) + (1,) * (len(extent) - dim - 1))

    gain = one(*cuts[0])
    for cut in cuts[1:]:
        gain = gain * one(*cut)
    return gain


def routed_block(rng, own, number, rows, count, top, limit, slope):
    ranking = jax.random.permutation(rng, count)
    packed, common = portions_of(count, rows * top, limit, slope, True), portions_of(count, rows * top, limit, slope, False)
    places = jnp.arange(count)

    def named(tallies, offset_by):
        used = int((tallies > 0).sum())
        fixed = max(1, used // 4)
        moved = fixed + (places - fixed + offset_by * (used - fixed)) % max(1, count - fixed)
        return jnp.zeros((count,), jnp.int32).at[ranking[jnp.where(places < fixed, places, moved)]].set(jnp.asarray(tallies, jnp.int32))

    tallies = jnp.where(number % 4 == 0, named(packed, number // 4), named(common, number - number // 4 - 1))
    mixed = jax.random.permutation(jax.random.fold_in(own, 3), count)
    donor, receiver = mixed[0:count // 2 * 2:2], mixed[1:count // 2 * 2:2]
    margin = jnp.minimum(tallies[donor] - 1, limit - tallies[receiver]) // 2
    margin = jnp.where((donor == ranking[0]) | (receiver == ranking[0]) | (tallies[receiver] == 0), 0, jnp.maximum(margin, 0))
    moved = jax.random.randint(jax.random.fold_in(own, 4), (count // 2,), 0, 1 << 20) % (margin + 1)
    tallies = tallies.at[donor].add(-moved).at[receiver].add(moved)
    members = jnp.searchsorted(jnp.cumsum(tallies), jnp.arange(rows * top), side="right").astype(jnp.int32)
    grid = members.reshape(top, rows).T
    grid = grid[jax.random.permutation(jax.random.fold_in(own, 1), rows)]
    offset_by = jax.random.randint(jax.random.fold_in(own, 2), (rows, 1), 0, top)
    return jnp.take_along_axis(grid, (jnp.arange(top)[None, :] + offset_by) % top, axis=1)


def portions_of(count, total, reach, slope, full):
    loads = [(1 << 20) // math.isqrt(standing ** slope) + 1 for standing in range(1, count + 1)]
    largest = reach if full else min(reach, max(-(-total // count), total * loads[0] // sum(loads)))
    least = 1 if total - largest >= count - 1 else 0
    given, surplus = [largest] + [least] * (count - 1), total - largest - least * (count - 1)
    while surplus > 0:
        free = [i for i in range(1, count) if given[i] < largest] or [i for i in range(1, count) if given[i] < reach]
        pool, budget = sum([loads[i] for i in free]), surplus
        for i in free:
            more = min(reach - given[i], max(1, budget * loads[i] // pool), surplus)
            given[i] = given[i] + more
            surplus = surplus - more
    return np.array(given)


def scatter_about(stream_key, extent, deviation, most, pieces=(), held_as=jnp.bfloat16):
    values = jax.random.normal(stream_key, extent, jnp.float32) * deviation
    if len(pieces) > 0:
        values = shard_levels(stream_key, extent, pieces, -0.22, 0.18) * values
    return jnp.clip(values, min=-most, max=most).astype(held_as)


def setup_inputs(seed: int = 0, part: int = 0) -> dict:
    key_list = jax.random.split(jax.random.key(seed), 8)
    part_splits = jax.random.split(jax.random.fold_in(key_list[7], part), 8)
    tokens = scatter_about(part_splits[0], (TOKENS, D), 1.0, 6.0, ((0, 8), (1, 2)))
    cotangent = scatter_about(part_splits[1], (TOKENS, D), 1.0, 6.0, ((0, 8), (1, 2)))
    expert_ids_keys = jax.random.split(jax.random.fold_in(part_splits[2], 1), TOKENS // TOK_DEV)
    expert_ids_turns = jax.random.permutation(jax.random.fold_in(part_splits[2], 3), TOKENS // TOK_DEV)
    expert_ids = jax.vmap(lambda own, number: routed_block(jax.random.fold_in(part_splits[2], 2), own, number, TOK_DEV, EXPERTS, TOP, CAP, 2))(expert_ids_keys, expert_ids_turns).reshape((TOKENS, TOP))
    gate_probs = jnp.clip(jnp.exp(math.log(1.0) - 2.9957323 * jax.random.uniform(part_splits[3], (TOKENS, TOP), jnp.float32) ** shard_levels(part_splits[3], (TOKENS, TOP), ((0, 8),), -0.2, 0.2)), 0.05, 1.0)
    w_gate = scatter_about(key_list[4], (EXPERTS, D, FF), D ** -0.5, 0.125, ((0, 4), (1, 2), (2, 2)))
    w_up = scatter_about(key_list[5], (EXPERTS, D, FF), D ** -0.5, 0.125, ((0, 4), (1, 2), (2, 2)))
    w_down = scatter_about(key_list[6], (EXPERTS, FF, D), FF ** -0.5, 0.15625, ((0, 4), (1, 2), (2, 2)))
    return {"tokens": tokens, "cotangent": cotangent, "expert_ids": expert_ids, "gate_probs": gate_probs, "w_gate": w_gate, "w_up": w_up, "w_down": w_down}


def reference(tokens, cotangent, expert_ids, gate_probs, w_gate, w_up, w_down):
    highest = lax.Precision.HIGHEST
    slot_total = TOKENS * TOP
    most_rows = N_DP * N_EXPERT * CAP
    flat_ids = expert_ids.reshape(-1).astype(jnp.int32)
    onehot = (flat_ids[:, None] == jnp.arange(EXPERTS, dtype=jnp.int32)[None, :]).astype(jnp.int32)
    position = jnp.sum((jnp.cumsum(onehot, axis=0) - onehot) * onehot, axis=1).astype(jnp.int32)
    row_table = jnp.full((EXPERTS, most_rows), slot_total, jnp.int32)
    row_table = row_table.at[flat_ids, position].set(jnp.arange(slot_total, dtype=jnp.int32))
    zero_row = jnp.zeros((1, D), jnp.bfloat16)
    token_slots = jnp.concatenate([jnp.repeat(tokens, TOP, axis=0), zero_row], axis=0)
    scaled = (gate_probs.reshape(-1, 1) * jnp.repeat(cotangent, TOP, axis=0).astype(jnp.float32)).astype(jnp.bfloat16)
    scaled_slots = jnp.concatenate([scaled, zero_row], axis=0)

    def per_expert(operands):
        row_index, gate_weight, up_weight, down_weight = operands
        rows_in = token_slots[row_index].astype(jnp.float32)
        cot_in = scaled_slots[row_index].astype(jnp.float32)
        gate_full = gate_weight.astype(jnp.float32)
        up_full = up_weight.astype(jnp.float32)
        down_full = down_weight.astype(jnp.float32)
        gate_act = jnp.dot(rows_in, gate_full, precision=highest)
        up_act = jnp.dot(rows_in, up_full, precision=highest)
        sigmoid_g = jax.nn.sigmoid(gate_act)
        hidden = (gate_act * sigmoid_g * up_act).astype(jnp.bfloat16)
        expert_out = jnp.dot(hidden.astype(jnp.float32), down_full, precision=highest).astype(jnp.bfloat16)
        split_cot = cot_in.reshape(-1, N_TENSOR, D // N_TENSOR)
        split_down = down_full.reshape(FF, N_TENSOR, D // N_TENSOR)
        partial_value = jnp.einsum("mjd,fjd->jmf", split_cot, split_down, precision=highest)
        hidden_grad = jnp.sum(lax.optimization_barrier(partial_value.astype(jnp.bfloat16)).astype(jnp.float32), axis=0)
        gate_grad = (hidden_grad * up_act * sigmoid_g * (1.0 + gate_act * (1.0 - sigmoid_g))).astype(jnp.bfloat16)
        up_grad = (hidden_grad * gate_act * sigmoid_g).astype(jnp.bfloat16)
        part_gate = jnp.einsum("mjf,djf->jmd", gate_grad.astype(jnp.float32).reshape(-1, N_TENSOR, FF // N_TENSOR),
                               gate_full.reshape(D, N_TENSOR, FF // N_TENSOR), precision=highest)
        part_up = jnp.einsum("mjf,djf->jmd", up_grad.astype(jnp.float32).reshape(-1, N_TENSOR, FF // N_TENSOR),
                             up_full.reshape(D, N_TENSOR, FF // N_TENSOR), precision=highest)
        summed = lax.optimization_barrier((part_gate + part_up).astype(jnp.bfloat16)).astype(jnp.float32)
        slot_grad = jnp.sum(summed, axis=0).astype(jnp.bfloat16)
        return expert_out, slot_grad

    out_rows, grad_rows = lax.map(per_expert, (row_table, w_gate, w_up, w_down))
    flat_table = row_table.reshape(-1)
    expert_out = jnp.zeros((slot_total + 1, D), jnp.bfloat16).at[flat_table].set(out_rows.reshape(-1, D))[:slot_total]
    slot_grad = jnp.zeros((slot_total + 1, D), jnp.bfloat16).at[flat_table].set(grad_rows.reshape(-1, D))[:slot_total]
    out_three = expert_out.reshape(TOKENS, TOP, D).astype(jnp.float32)
    layer_out = jnp.sum(gate_probs[:, :, None] * out_three, axis=1).astype(jnp.bfloat16)
    grad_tokens = jnp.sum(slot_grad.reshape(TOKENS, TOP, D).astype(jnp.float32), axis=1).astype(jnp.bfloat16)
    grad_probs = jnp.sum(out_three * cotangent[:, None, :].astype(jnp.float32), axis=2)
    return layer_out, grad_tokens, grad_probs
```

```python
import functools

import jax
import jax.numpy as jnp
from jax import lax
from jax.experimental import pallas as pl
from jax.experimental.pallas import tpu as pltpu
from jax.sharding import PartitionSpec as P

F32 = jnp.float32
BF16 = jnp.bfloat16
LAST = (((1,), (1,)), ((), ()))
ROW_CHUNKS = 2
COL_CHUNKS = 2
SHIFTED_UP_TO = 8

VMEM = pl.BlockSpec(memory_space=pltpu.VMEM)
SMEM = pl.BlockSpec(memory_space=pltpu.SMEM)
ANY = pl.BlockSpec(memory_space=pl.ANY)


def dot(a, b, dims=(((1,), (0,)), ((), ()))):
    return lax.dot_general(a, b, dims, preferred_element_type=F32)


def call(kernel, out_shape, args, spaces, scratch=(), flops=0, moved=0):
    return pl.pallas_call(
        kernel,
        out_shape=out_shape,
        in_specs=spaces,
        out_specs=jax.tree.map(lambda _: VMEM, out_shape),
        scratch_shapes=list(scratch),
        compiler_params=pltpu.CompilerParams(vmem_limit_bytes=40 * 1024 * 1024),
        cost_estimate=pl.CostEstimate(flops=flops, bytes_accessed=moved, transcendentals=0),
    )(*args)


def shape(rows, cols, dtype):
    return jax.ShapeDtypeStruct((rows, cols), dtype)


def padded(size):
    return -(-size // 128) * 128


class Copies:
    def __init__(self, sems):
        self.sems, self.all = sems, []

    def add(self, src, dst):
        copy = pltpu.make_async_copy(src, dst, self.sems.at[len(self.all)])
        copy.start()
        self.all.append(copy)

    def wait(self):
        for copy in self.all:
            copy.wait()


def before(index, step, size):
    moved = index - step
    return jnp.where(moved < 0, moved + size, moved)


def rows_at(start, size):
    return pl.ds(pl.multiple_of(start, 16), size)


def cols_at(start, size):
    return pl.ds(pl.multiple_of(start, 128), size)


def route_kernel(experts, cap, blocks, where, ids_t, probs_t, ids, tok, cot, *outs):
    tok_out, cot_out = outs[:blocks], outs[blocks : 2 * blocks]
    first_out, second_out = outs[2 * blocks :]
    rows, count = experts * cap, tok.shape[0]
    base = where[1] if blocks > 1 else 0

    def places(axis):
        row = lax.broadcasted_iota(jnp.int32, (rows, 1) if axis == 0 else (1, rows), axis)
        block = jnp.zeros_like(row)
        for later in range(1, experts):
            block = block + (row >= later * cap).astype(jnp.int32)
        expert = block + base
        expert = jnp.where(expert >= experts, expert - experts, expert)
        return expert, (row - block * cap).astype(F32)

    side = (lax.broadcasted_iota(jnp.int32, (count, count), 0), lax.broadcasted_iota(jnp.int32, (count, count), 1))
    expert, slot = places(0)
    first = ids_t[0:1, :] == expert
    named = first | (ids_t[1:2, :] == expert)
    earlier = dot(named.astype(F32).astype(BF16), (side[0] < side[1]).astype(F32).astype(BF16))
    chosen = named & (earlier == slot)
    weight = jnp.where(chosen, jnp.where(first, probs_t[0:1, :], probs_t[1:2, :]), 0.0)
    weight = jnp.sum(weight, axis=1, keepdims=True)
    chosen = chosen.astype(F32).astype(BF16)
    tok_rows = dot(chosen, tok[...]).astype(BF16)
    cot_rows = (weight * dot(chosen, cot[...])).astype(BF16)
    each = rows // blocks
    for i in range(blocks):
        tok_out[i][...] = tok_rows[i * each : (i + 1) * each]
        cot_out[i][...] = cot_rows[i * each : (i + 1) * each]

    expert, slot = places(1)
    first = ids[:, 0:1] == expert
    second = ids[:, 1:2] == expert
    named = (first | second).astype(F32).astype(BF16)
    earlier = dot((side[1] < side[0]).astype(F32).astype(BF16), named)
    here = earlier == slot
    first_out[...] = (first & here).astype(F32).astype(BF16)
    second_out[...] = (second & here).astype(F32).astype(BF16)


def fill_tokens(where, copies, own, other, dst):
    half = own[0].shape[1]
    at = 0
    for i in range(len(own)):
        rows = own[i].shape[0]
        copies.add(own[i], dst.at[pl.ds(at, rows), cols_at(where[3] * half, half)])
        copies.add(other[i], dst.at[pl.ds(at, rows), cols_at((1 - where[3]) * half, half)])
        at += rows


def fill_wide(where, copies, sizes, own, pieces, dst):
    n_dp, n_groups = sizes
    units, feats = own.shape
    copies.add(own, dst.at[pl.ds(0, units), cols_at(where[2] * feats, feats)])
    share = units // n_groups
    for (chunk, step, turn), ref in pieces:
        start = before(where[0], turn, n_groups) * share + chunk * ref.shape[0]
        feat = before(where[2], step, n_dp) * feats
        copies.add(ref, dst.at[rows_at(start, ref.shape[0]), cols_at(feat, feats)])
    if dst.shape[0] > units:
        dst[units:, :] = jnp.zeros((dst.shape[0] - units, dst.shape[1]), dst.dtype)


def fill_down(where, copies, sizes, own, pieces, parts, dst):
    n_dp, n_groups = sizes
    units, feats = own.shape
    half = dst.shape[0] // 2
    per_half = n_dp // 2
    share = feats // n_groups
    width = share // COL_CHUNKS

    def start(index):
        upper = (index >= per_half).astype(jnp.int32)
        return upper * half + (index - upper * per_half) * units

    for place, part in enumerate(parts):
        for group in range(n_groups):
            copies.add(
                own.at[:, pl.ds(group * share + part * width, width)],
                dst.at[rows_at(start(where[2]), units), pl.ds((place * n_groups + group) * width, width)],
            )
    for (part, step, turn), ref in pieces:
        col = (parts.index(part) * n_groups + before(where[0], turn, n_groups)) * width
        copies.add(ref, dst.at[rows_at(start(before(where[2], step, n_dp)), units), cols_at(col, width)])
    used = per_half * units
    if half > used:
        for side in range(2):
            dst[side * half + used : (side + 1) * half, :] = jnp.zeros((half - used, dst.shape[1]), dst.dtype)


def front_kernel(sizes, keys, blocks, final, where, *refs):
    own_tok, other_tok, refs = refs[:blocks], refs[blocks : 2 * blocks], refs[2 * blocks :]
    own, refs = refs[0], refs[1:]
    pieces, refs = list(zip(keys, refs[: len(keys)])), refs[len(keys) :]
    if final:
        gate, up_out, hidden_out, tok, weight, sems = refs
    else:
        gate_out, tok, weight, sems = refs
    copies = Copies(sems)
    fill_tokens(where, copies, own_tok, other_tok, tok)
    fill_wide(where, copies, sizes, own, pieces, weight)
    copies.wait()
    value = dot(tok[...], weight[...], LAST)
    if final:
        up_out[...] = value
        hidden_out[...] = (gate[...] * jax.nn.sigmoid(gate[...]) * value).astype(BF16)
    else:
        gate_out[...] = value


def out_kernel(sizes, keys, part, where, own_hidden, other_hidden, own, *refs):
    pieces, refs = list(zip(keys, refs[: len(keys)])), refs[len(keys) :]
    outs, (hidden, weight, sems) = refs[:-3], refs[-3:]
    copies = Copies(sems)
    half = own_hidden.shape[1]
    copies.add(own_hidden, hidden.at[:, cols_at(where[3] * half, half)])
    copies.add(other_hidden, hidden.at[:, cols_at((1 - where[3]) * half, half)])
    fill_down(where, copies, sizes, own, pieces, [part], weight)
    copies.wait()
    value = dot(hidden[...], weight[...]).astype(BF16)
    each = outs[0].shape[0]
    for i, out in enumerate(outs):
        out[...] = value[i * each : (i + 1) * each]


def cot_kernel(sizes, keys, blocks, where, *refs):
    cots, own, refs = refs[:blocks], refs[blocks], refs[blocks + 1 :]
    pieces, refs = list(zip(keys, refs[: len(keys)])), refs[len(keys) :]
    keep, send, cot, weight, sems = refs
    copies = Copies(sems)
    share = own.shape[1] // sizes[1]
    width = share // COL_CHUNKS
    at = 0
    for ref in cots:
        rows = ref.shape[0]
        for part in range(COL_CHUNKS):
            for group in range(sizes[1]):
                copies.add(
                    ref.at[:, pl.ds(group * share + part * width, width)],
                    cot.at[pl.ds(at, rows), pl.ds((part * sizes[1] + group) * width, width)],
                )
        at += rows
    fill_down(where, copies, sizes, own, pieces, list(range(COL_CHUNKS)), weight)
    copies.wait()
    half = weight.shape[0] // 2
    send[...] = dot(cot[...], weight[rows_at((1 - where[3]) * half, half), :], LAST).astype(BF16)
    keep[...] = dot(cot[...], weight[rows_at(where[3] * half, half), :], LAST)


def grad_kernel(sizes, gate_keys, up_keys, where, gate, up, kept, received, own_gate, own_up, *refs):
    gate_pieces = list(zip(gate_keys, refs[: len(gate_keys)]))
    refs = refs[len(gate_keys) :]
    up_pieces = list(zip(up_keys, refs[: len(up_keys)]))
    keep, send, w_gate, w_up, sems = refs[len(up_keys) :]
    copies = Copies(sems)
    fill_wide(where, copies, sizes, own_gate, gate_pieces, w_gate)
    fill_wide(where, copies, sizes, own_up, up_pieces, w_up)
    gate_act = gate[...]
    sigmoid_g = jax.nn.sigmoid(gate_act)
    hidden_grad = kept[...] + received[...].astype(F32)
    gate_grad = (hidden_grad * up[...] * sigmoid_g * (1.0 + gate_act * (1.0 - sigmoid_g))).astype(BF16)
    up_grad = (hidden_grad * gate_act * sigmoid_g).astype(BF16)
    copies.wait()
    half = keep.shape[1]
    mine, theirs = cols_at(where[3] * half, half), cols_at((1 - where[3]) * half, half)
    send[...] = (dot(gate_grad, w_gate[:, theirs]) + dot(up_grad, w_up[:, theirs])).astype(BF16)
    keep[...] = dot(gate_grad, w_gate[:, mine]) + dot(up_grad, w_up[:, mine])


def add_kernel(kept, received, *outs):
    value = (kept[...] + received[...].astype(F32)).astype(BF16)
    each = outs[0].shape[0]
    for i, out in enumerate(outs):
        out[...] = value[i * each : (i + 1) * each]


def layer_kernel(blocks, n_groups, first, second, probs, cot, *refs):
    out, prob_out = refs[-2:]
    share = cot.shape[1] // n_groups
    width = share // COL_CHUNKS
    sums = [0.0, 0.0]
    for part in range(COL_CHUNKS):
        back = jnp.concatenate([r[...] for r in refs[part * blocks : (part + 1) * blocks]], axis=0)
        slots = dot(first[...], back), dot(second[...], back)
        total = probs[:, 0:1] * slots[0] + probs[:, 1:2] * slots[1]
        for group in range(n_groups):
            cols = pl.ds(group * share + part * width, width)
            out[:, cols] = total[:, group * width : (group + 1) * width].astype(BF16)
            cot_here = cot[:, cols].astype(F32)
            for k in range(2):
                held = slots[k][:, group * width : (group + 1) * width] * cot_here
                sums[k] = sums[k] + jnp.sum(held, axis=1, keepdims=True)
    lane = lax.broadcasted_iota(jnp.int32, prob_out.shape, 1)
    prob_out[...] = jnp.where(lane == 0, sums[0], sums[1])


def token_kernel(first, second, *refs):
    back = jnp.concatenate([r[...] for r in refs[:-1]], axis=0)
    refs[-1][...] = dot(first[...] + second[...], back).astype(BF16)


def shift(value, axis, step):
    size = lax.axis_size(axis)
    return lax.ppermute(value, axis, [(i, (i + step) % size) for i in range(size)])


def local(tokens, cotangent, expert_ids, gate_probs, w_gate, w_up, w_down):
    count, half = tokens.shape
    experts, n_dp, n_groups = lax.axis_size("expert"), lax.axis_size("dp"), lax.axis_size("groups")
    sizes = (n_dp, n_groups)
    cap = 3 * count * expert_ids.shape[1] // (2 * experts)
    rows = experts * cap
    shifted = experts <= SHIFTED_UP_TO
    blocks = experts if shifted else 1
    each = rows // blocks
    group = lax.axis_index("groups")
    where = jnp.stack([lax.axis_index(a) for a in ("groups", "expert", "dp", "tensor")]).astype(jnp.int32)

    def exchange(parts, sign):
        if shifted:
            return [parts[0]] + [shift(parts[s], "expert", sign * s) for s in range(1, experts)]
        whole = parts[0].reshape(experts, cap, -1)
        whole = lax.all_to_all(whole, "expert", split_axis=0, concat_axis=0, tiled=True)
        return [whole.reshape(rows, -1)]

    def gather(weight, axis, chunks):
        share = weight.shape[axis] // n_groups
        size = share // chunks
        keys, pieces = [], []
        for chunk in range(chunks):
            mine = lax.dynamic_slice_in_dim(weight, group * share + chunk * size, size, axis)
            for step in range(1, n_dp):
                came = shift(mine, "dp", step)
                for turn in range(n_groups):
                    keys.append((chunk, step, turn))
                    pieces.append(shift(came, "groups", turn) if turn else came)
        return keys, pieces

    gate_t, up_t, down = jnp.swapaxes(w_gate[0], 0, 1), jnp.swapaxes(w_up[0], 0, 1), w_down[0]
    units = gate_t.shape[0]
    wide = padded(units)
    feats = n_dp * gate_t.shape[1]
    gate_keys, gate_pieces = gather(gate_t, 0, ROW_CHUNKS)

    routed = call(
        functools.partial(route_kernel, experts, cap, blocks),
        [shape(each, half, BF16)] * (2 * blocks) + [shape(count, rows, BF16)] * 2,
        (where, expert_ids.T, gate_probs.T, expert_ids, tokens, cotangent),
        [SMEM] + [VMEM] * 5,
        flops=4 * rows * count * half,
        moved=4 * count * half + 4 * rows * half,
    )
    first, second = routed[2 * blocks :]
    tok = exchange(routed[:blocks], 1)
    cot = exchange(routed[blocks : 2 * blocks], 1)
    other_tok = [shift(part, "tensor", 1) for part in tok]
    up_keys, up_pieces = gather(up_t, 0, ROW_CHUNKS)
    down_keys, down_pieces = gather(down, 1, COL_CHUNKS)

    def front(own, keys, pieces, gate):
        final = gate is not None
        act = shape(rows, wide, F32)
        return call(
            functools.partial(front_kernel, sizes, keys, blocks, final),
            [act, shape(rows, wide, BF16)] if final else [act],
            (where, *tok, *other_tok, own, *pieces, *([gate] if final else [])),
            [SMEM] + [ANY] * (2 * blocks + 1 + len(pieces)) + [VMEM] * final,
            [
                pltpu.VMEM((rows, feats), BF16),
                pltpu.VMEM((wide, feats), BF16),
                pltpu.SemaphoreType.DMA((2 * blocks + 1 + len(pieces),)),
            ],
            flops=2 * rows * feats * units,
            moved=2 * feats * (rows + units),
        )

    (gate,) = front(gate_t, gate_keys, gate_pieces, None)
    up, hidden = front(up_t, up_keys, up_pieces, gate)
    other_hidden = shift(hidden, "tensor", 1)

    width = half // n_groups // COL_CHUNKS
    back = []
    for part in range(COL_CHUNKS):
        picked = [i for i, key in enumerate(down_keys) if key[0] == part]
        outs = call(
            functools.partial(out_kernel, sizes, [down_keys[i] for i in picked], part),
            [shape(each, n_groups * width, BF16)] * blocks,
            (where, hidden, other_hidden, down, *[down_pieces[i] for i in picked]),
            [SMEM] + [ANY] * (3 + len(picked)),
            [
                pltpu.VMEM((rows, 2 * wide), BF16),
                pltpu.VMEM((2 * wide, n_groups * width), BF16),
                pltpu.SemaphoreType.DMA((2 + n_groups + len(picked),)),
            ],
            flops=4 * rows * units * n_groups * width,
            moved=4 * units * n_groups * width,
        )
        back.append(exchange(outs, -1))

    kept, sent = call(
        functools.partial(cot_kernel, sizes, down_keys, blocks),
        [shape(rows, wide, F32), shape(rows, wide, BF16)],
        (where, *cot, down, *down_pieces),
        [SMEM] + [ANY] * (blocks + 1 + len(down_pieces)),
        [
            pltpu.VMEM((rows, half), BF16),
            pltpu.VMEM((2 * wide, half), BF16),
            pltpu.SemaphoreType.DMA((COL_CHUNKS * n_groups * (blocks + 1) + len(down_pieces),)),
        ],
        flops=4 * rows * half * units,
        moved=4 * half * units,
    )
    received = shift(sent, "tensor", 1)
    kept, sent = call(
        functools.partial(grad_kernel, sizes, gate_keys, up_keys),
        [shape(rows, half, F32), shape(rows, half, BF16)],
        (where, gate, up, kept, received, gate_t, up_t, *gate_pieces, *up_pieces),
        [SMEM] + [VMEM] * 4 + [ANY] * (2 + len(gate_pieces) + len(up_pieces)),
        [
            pltpu.VMEM((wide, feats), BF16),
            pltpu.VMEM((wide, feats), BF16),
            pltpu.SemaphoreType.DMA((2 + len(gate_pieces) + len(up_pieces),)),
        ],
        flops=4 * rows * feats * units,
        moved=4 * feats * units,
    )
    received = shift(sent, "tensor", 1)
    slots = call(add_kernel, [shape(each, half, BF16)] * blocks, (kept, received), [VMEM] * 2, moved=8 * rows * half)
    grad_back = exchange(slots, -1)

    layer_out, prob_part = call(
        functools.partial(layer_kernel, blocks, n_groups),
        [shape(count, half, BF16), shape(count, expert_ids.shape[1], F32)],
        (first, second, gate_probs, cotangent, *[part for parts in back for part in parts]),
        [VMEM] * (4 + COL_CHUNKS * blocks),
        flops=4 * count * rows * half,
        moved=2 * rows * half,
    )
    grad_probs = prob_part + shift(prob_part, "tensor", 1)
    (grad_tokens,) = call(
        token_kernel,
        [shape(count, half, BF16)],
        (first, second, *grad_back),
        [VMEM] * (2 + blocks),
        flops=2 * count * rows * half,
        moved=2 * rows * half,
    )
    return (layer_out, grad_tokens, grad_probs)


def solution(mesh):
    by_token = ("groups", "expert", "dp")
    weight = P("expert", "dp", "tensor")
    in_specs = (P(by_token, "tensor"), P(by_token, "tensor"), P(by_token, None), P(by_token, None)) + (weight,) * 3
    out_specs = (P(by_token, "tensor"), P(by_token, "tensor"), P(by_token, None))
    return jax.shard_map(local, mesh=mesh, in_specs=in_specs, out_specs=out_specs, check_vma=False)
```

```python
import functools

import jax
import jax.numpy as jnp
from jax import lax
from jax.experimental import pallas as pl
from jax.experimental.pallas import tpu as pltpu
from jax.sharding import PartitionSpec as P

F32 = jnp.float32
BF16 = jnp.bfloat16
LAST = (((1,), (1,)), ((), ()))
ROW_CHUNKS = 2
COL_CHUNKS = 2
WHOLE = 60
SHIFTED_UP_TO = 8

VMEM = pl.BlockSpec(memory_space=pltpu.VMEM)
SMEM = pl.BlockSpec(memory_space=pltpu.SMEM)
ANY = pl.BlockSpec(memory_space=pl.ANY)
HBM = pl.BlockSpec(memory_space=pltpu.HBM)


def dot(a, b, dims=(((1,), (0,)), ((), ()))):
    return lax.dot_general(a, b, dims, preferred_element_type=F32)


def call(kernel, out_shape, args, spaces, scratch=(), flops=0, moved=0, outs=VMEM, grant=40):
    return pl.pallas_call(
        kernel,
        out_shape=out_shape,
        in_specs=spaces,
        out_specs=jax.tree.map(lambda _: outs, out_shape),
        scratch_shapes=list(scratch),
        compiler_params=pltpu.CompilerParams(vmem_limit_bytes=grant * 1024 * 1024),
        cost_estimate=pl.CostEstimate(flops=flops, bytes_accessed=moved, transcendentals=0),
    )(*args)


def shape(rows, cols, dtype):
    return jax.ShapeDtypeStruct((rows, cols), dtype)


def padded(size):
    return -(-size // 128) * 128


class Copies:
    def __init__(self, sems):
        self.sems, self.all = sems, []

    def add(self, src, dst):
        copy = pltpu.make_async_copy(src, dst, self.sems.at[len(self.all)])
        copy.start()
        self.all.append(copy)

    def wait(self):
        for copy in self.all:
            copy.wait()


def before(index, step, size):
    moved = index - step
    return jnp.where(moved < 0, moved + size, moved)


def rows_at(start, size):
    return pl.ds(pl.multiple_of(start, 16), size)


def cols_at(start, size):
    return pl.ds(pl.multiple_of(start, 128), size)


def places(experts, cap, blocks, where, ids_t):
    rows, count = experts * cap, ids_t.shape[1]
    row = lax.broadcasted_iota(jnp.int32, (rows, 1), 0)
    block = jnp.zeros_like(row)
    for later in range(1, experts):
        block = block + (row >= later * cap).astype(jnp.int32)
    expert = block + (where[1] if blocks > 1 else 0)
    expert = jnp.where(expert >= experts, expert - experts, expert)
    slot = (row - block * cap).astype(F32)
    first = ids_t[0:1, :] == expert
    second = ids_t[1:2, :] == expert
    before_it = lax.broadcasted_iota(jnp.int32, (count, count), 0) < lax.broadcasted_iota(jnp.int32, (count, count), 1)
    earlier = dot((first | second).astype(F32).astype(BF16), before_it.astype(F32).astype(BF16))
    here = earlier == slot
    return first & here, second & here


def route_kernel(experts, cap, blocks, where, ids_in, probs_in, tok_in, cot_in, *refs):
    tok_out, cot_out = refs[:blocks], refs[blocks : 2 * blocks]
    ids_t, probs_t, tok, cot, sems = refs[2 * blocks :]
    copies = Copies(sems)
    copies.add(ids_in, ids_t)
    copies.add(probs_in, probs_t)
    copies.add(tok_in, tok)
    copies.add(cot_in, cot)
    copies.wait()
    first, second = places(experts, cap, blocks, where, ids_t)
    weight = jnp.where(first, probs_t[0:1, :], jnp.where(second, probs_t[1:2, :], 0.0))
    weight = jnp.sum(weight, axis=1, keepdims=True)
    chosen = (first | second).astype(F32).astype(BF16)
    tok_rows = dot(chosen, tok[...]).astype(BF16)
    cot_rows = (weight * dot(chosen, cot[...])).astype(BF16)
    each = tok_rows.shape[0] // blocks
    for i in range(blocks):
        tok_out[i][...] = tok_rows[i * each : (i + 1) * each]
        cot_out[i][...] = cot_rows[i * each : (i + 1) * each]


def cut_kernel(axis, chunk, n_groups, where, weight, *refs):
    out, sems = refs[-2:]
    share = weight.shape[axis] // n_groups
    start, size = where[0] * share + chunk * out.shape[axis], out.shape[axis]
    copies = Copies(sems)
    copies.add(weight.at[rows_at(start, size), :] if axis == 0 else weight.at[:, cols_at(start, size)], out)
    copies.wait()


def join_kernel(*refs):
    parts, out, sems = refs[:-2], refs[-2], refs[-1]
    copies, at = Copies(sems), 0
    for part in parts:
        copies.add(part, out.at[pl.ds(at, part.shape[0]), :])
        at += part.shape[0]
    copies.wait()


def after_kernel(*refs):
    pass


def after(value, *others):
    return pl.pallas_call(
        after_kernel,
        out_shape=jax.ShapeDtypeStruct(value.shape, value.dtype),
        in_specs=[ANY] * (1 + len(others)),
        out_specs=ANY,
        input_output_aliases={0: 0},
    )(value, *others)


def fill_tokens(where, copies, own, other, dst):
    half = own.shape[1]
    copies.add(own, dst.at[:, cols_at(where[3] * half, half)])
    copies.add(other, dst.at[:, cols_at((1 - where[3]) * half, half)])


def fill_wide(where, copies, sizes, own, pieces, dst):
    n_dp, n_groups = sizes
    units, feats = own.shape
    copies.add(own, dst.at[pl.ds(0, units), cols_at(where[2] * feats, feats)])
    share = units // n_groups
    for (chunk, step, turn), ref in pieces:
        start = before(where[0], turn, n_groups) * share + chunk * ref.shape[0]
        feat = before(where[2], step, n_dp) * feats
        copies.add(ref, dst.at[rows_at(start, ref.shape[0]), cols_at(feat, feats)])
    if dst.shape[0] > units:
        dst[units:, :] = jnp.zeros((dst.shape[0] - units, dst.shape[1]), dst.dtype)


def fill_down(where, copies, sizes, own, pieces, parts, dst):
    n_dp, n_groups = sizes
    units, feats = own.shape
    half = dst.shape[0] // 2
    per_half = n_dp // 2
    share = feats // n_groups
    width = share // COL_CHUNKS

    def start(index):
        upper = (index >= per_half).astype(jnp.int32)
        return upper * half + (index - upper * per_half) * units

    for place, part in enumerate(parts):
        for group in range(n_groups):
            copies.add(
                own.at[:, pl.ds(group * share + part * width, width)],
                dst.at[rows_at(start(where[2]), units), pl.ds((place * n_groups + group) * width, width)],
            )
    for (part, step, turn), ref in pieces:
        col = (parts.index(part) * n_groups + before(where[0], turn, n_groups)) * width
        copies.add(ref, dst.at[rows_at(start(before(where[2], step, n_dp)), units), cols_at(col, width)])
    used = per_half * units
    if half > used:
        for side in range(2):
            dst[side * half + used : (side + 1) * half, :] = jnp.zeros((half - used, dst.shape[1]), dst.dtype)


def front_kernel(sizes, keys, final, where, own_tok, other_tok, own, *refs):
    pieces, refs = list(zip(keys, refs[: len(keys)])), refs[len(keys) :]
    if final:
        gate, (up_out, hidden_out, tok, weight, sems) = refs[0], refs[-5:]
    else:
        gate_out, tok, weight, sems = refs
    copies = Copies(sems)
    fill_tokens(where, copies, own_tok, other_tok, tok)
    fill_wide(where, copies, sizes, own, pieces, weight)
    copies.wait()
    value = dot(tok[...], weight[...], LAST)
    if final:
        up_out[...] = value
        hidden_out[...] = (gate[...] * jax.nn.sigmoid(gate[...]) * value).astype(BF16)
    else:
        gate_out[...] = value


def out_kernel(sizes, keys, part, blocks, where, own_hidden, other_hidden, own, *refs):
    pieces = list(zip(keys, refs[: len(keys)]))
    outs, (hidden, weight, sems) = refs[-3 - blocks : -3], refs[-3:]
    copies = Copies(sems)
    half = own_hidden.shape[1]
    copies.add(own_hidden, hidden.at[:, cols_at(where[3] * half, half)])
    copies.add(other_hidden, hidden.at[:, cols_at((1 - where[3]) * half, half)])
    fill_down(where, copies, sizes, own, pieces, [part], weight)
    copies.wait()
    value = dot(hidden[...], weight[...]).astype(BF16)
    each = outs[0].shape[0]
    for i, out in enumerate(outs):
        out[...] = value[i * each : (i + 1) * each]


def cot_kernel(sizes, keys, blocks, where, *refs):
    cots, own, refs = refs[:blocks], refs[blocks], refs[blocks + 1 :]
    pieces, refs = list(zip(keys, refs[: len(keys)])), refs[len(keys) :]
    keep, send, cot, weight, sems = refs[1:]
    copies = Copies(sems)
    share = own.shape[1] // sizes[1]
    width = share // COL_CHUNKS
    at = 0
    for ref in cots:
        rows = ref.shape[0]
        for part in range(COL_CHUNKS):
            for group in range(sizes[1]):
                copies.add(
                    ref.at[:, pl.ds(group * share + part * width, width)],
                    cot.at[pl.ds(at, rows), pl.ds((part * sizes[1] + group) * width, width)],
                )
        at += rows
    fill_down(where, copies, sizes, own, pieces, list(range(COL_CHUNKS)), weight)
    copies.wait()
    half = weight.shape[0] // 2
    send[...] = dot(cot[...], weight[rows_at((1 - where[3]) * half, half), :], LAST).astype(BF16)
    keep[...] = dot(cot[...], weight[rows_at(where[3] * half, half), :], LAST)


def grad_kernel(sizes, gate_keys, up_keys, where, gate, up, kept, received, own_gate, own_up, *refs):
    gate_pieces = list(zip(gate_keys, refs[: len(gate_keys)]))
    refs = refs[len(gate_keys) :]
    up_pieces = list(zip(up_keys, refs[: len(up_keys)]))
    keep, send, w_gate, w_up, sems = refs[-5:]
    copies = Copies(sems)
    fill_wide(where, copies, sizes, own_gate, gate_pieces, w_gate)
    fill_wide(where, copies, sizes, own_up, up_pieces, w_up)
    gate_act = gate[...]
    sigmoid_g = jax.nn.sigmoid(gate_act)
    hidden_grad = kept[...] + received[...].astype(F32)
    gate_grad = (hidden_grad * up[...] * sigmoid_g * (1.0 + gate_act * (1.0 - sigmoid_g))).astype(BF16)
    up_grad = (hidden_grad * gate_act * sigmoid_g).astype(BF16)
    copies.wait()
    half = keep.shape[1]
    mine, theirs = cols_at(where[3] * half, half), cols_at((1 - where[3]) * half, half)
    send[...] = (dot(gate_grad, w_gate[:, theirs]) + dot(up_grad, w_up[:, theirs])).astype(BF16)
    keep[...] = dot(gate_grad, w_gate[:, mine]) + dot(up_grad, w_up[:, mine])


def add_kernel(kept, received, *outs):
    value = (kept[...] + received[...].astype(F32)).astype(BF16)
    each = outs[0].shape[0]
    for i, out in enumerate(outs):
        out[...] = value[i * each : (i + 1) * each]


def layer_kernel(experts, cap, blocks, n_groups, where, ids_t, probs_t, cot, *refs):
    out, prob_out, both_out = refs[-3:]
    share = cot.shape[1] // n_groups
    width = share // COL_CHUNKS
    sums = [0.0, 0.0]
    first, second = (m.astype(F32).T.astype(BF16) for m in places(experts, cap, blocks, where, ids_t))
    both_out[...] = first + second
    probs = jnp.concatenate([probs_t[...], jnp.zeros((6, probs_t.shape[1]), F32)], axis=0).T
    for part in range(COL_CHUNKS):
        back = jnp.concatenate([r[...] for r in refs[part * blocks : (part + 1) * blocks]], axis=0)
        slots = dot(first, back), dot(second, back)
        total = probs[:, 0:1] * slots[0] + probs[:, 1:2] * slots[1]
        for group in range(n_groups):
            cols = pl.ds(group * share + part * width, width)
            out[:, cols] = total[:, group * width : (group + 1) * width].astype(BF16)
            cot_here = cot[:, cols].astype(F32)
            for k in range(2):
                held = slots[k][:, group * width : (group + 1) * width] * cot_here
                sums[k] = sums[k] + jnp.sum(held, axis=1, keepdims=True)
    lane = lax.broadcasted_iota(jnp.int32, (cot.shape[0], 128), 1)
    prob_out[...] = jnp.where(lane == 0, sums[0], sums[1]).T[0:2, :]


def token_kernel(both, *refs):
    back = jnp.concatenate([r[...] for r in refs[:-1]], axis=0)
    refs[-1][...] = dot(both[...], back).astype(BF16)


def shift(value, axis, step):
    size = lax.axis_size(axis)
    return lax.ppermute(value, axis, [(i, (i + step) % size) for i in range(size)])


def local(tokens, cotangent, expert_ids, gate_probs, w_gate, w_up, w_down):
    count, half = tokens.shape
    experts, n_dp, n_groups = lax.axis_size("expert"), lax.axis_size("dp"), lax.axis_size("groups")
    sizes = (n_dp, n_groups)
    cap = 3 * count * expert_ids.shape[1] // (2 * experts)
    rows = experts * cap
    shifted = experts <= SHIFTED_UP_TO
    blocks = experts if shifted else 1
    each = rows // blocks
    group = lax.axis_index("groups")
    where = jnp.stack([lax.axis_index(a) for a in ("groups", "expert", "dp", "tensor")]).astype(jnp.int32)

    def exchange(parts, sign):
        whole = parts[0].reshape(experts, cap, -1)
        whole = lax.all_to_all(whole, "expert", split_axis=0, concat_axis=0, tiled=True)
        return [whole.reshape(rows, -1)]

    order = [experts // 2] + [s for s in range(1, experts) if s != experts // 2]

    def travel(parts, sign, earlier=(), held=(), seen=None):
        if not shifted:
            came = exchange(parts, sign)
            if seen is not None:
                seen.extend(came * 3)
            return came
        came = list(parts)
        for i, s in enumerate(order):
            wait = [earlier[s]] if len(earlier) else []
            wait += list(held[i]()) if i < len(held) else []
            came[s] = shift(after(parts[s], *wait) if wait else parts[s], "expert", sign * s)
            if seen is not None:
                seen.append(came[s])
        return came

    cuts = []

    def cut(i, *held):
        weight, axis, chunk = plan[i]
        size = weight.shape[axis] // n_groups // (COL_CHUNKS if axis else ROW_CHUNKS)
        mine = call(
            functools.partial(cut_kernel, axis, chunk, n_groups),
            shape(weight.shape[0] if axis else size, size if axis else weight.shape[1], BF16),
            (where, weight, *held, *cuts[-1:]),
            [SMEM, HBM] + [ANY] * (len(held) + len(cuts[-1:])),
            [pltpu.SemaphoreType.DMA((1,))],
            outs=ANY,
            grant=WHOLE,
        )
        cuts.append(mine)
        return [shift(mine, "dp", step) for step in range(1, n_dp)]

    def turn_over(i, came, *held):
        keys, pieces = [], []
        for step, here in enumerate(came, 1):
            here = after(here, *held) if held else here
            for turn in range(n_groups):
                keys.append((plan[i][2], step, turn))
                pieces.append(shift(here, "groups", turn) if turn else here)
        return keys, pieces

    gate_t, up_t, down = jnp.swapaxes(w_gate[0], 0, 1), jnp.swapaxes(w_up[0], 0, 1), w_down[0]
    units = gate_t.shape[0]
    wide = padded(units)
    feats = n_dp * gate_t.shape[1]
    plan = [(gate_t, 0, c) for c in range(ROW_CHUNKS)] + [(up_t, 0, c) for c in range(ROW_CHUNKS)]
    plan += [(down, 1, c) for c in range(COL_CHUNKS)]
    x = {0: cut(0), 1: cut(1)}
    y = {}

    routed = call(
        functools.partial(route_kernel, experts, cap, blocks),
        [shape(each, half, BF16)] * (2 * blocks),
        (where, expert_ids.T, gate_probs.T, tokens, cotangent),
        [SMEM] + [HBM] * 4,
        [
            pltpu.VMEM(expert_ids.T.shape, jnp.int32),
            pltpu.VMEM(gate_probs.T.shape, F32),
            pltpu.VMEM(tokens.shape, BF16),
            pltpu.VMEM(cotangent.shape, BF16),
            pltpu.SemaphoreType.DMA((4,)),
        ],
        grant=WHOLE,
        flops=4 * rows * count * half,
        moved=4 * count * half + 4 * rows * half,
    )
    seen, cot_seen = [], []
    tok = travel(routed[:blocks], 1, held=[lambda: (), lambda: (seen[0], x[0][-1]), lambda: (seen[1], x[1][-1])], seen=seen)
    y[0] = turn_over(0, x[0])
    x[2] = cut(2, x[0][-1])
    y[1] = turn_over(1, x[1])
    x[3] = cut(3, x[1][-1], seen[1])
    cot_held = [lambda: (seen[-1], x[2][-1]), lambda: cot_seen[:1], lambda: cot_seen[1:2]]
    cot = travel(list(routed[blocks:]), 1, held=cot_held, seen=cot_seen)
    y[2] = turn_over(2, x[2], y[0][1][-1])
    x[4] = cut(4, x[2][-1], seen[-1])
    y[3] = turn_over(3, x[3], y[1][1][-1])
    x[5] = cut(5, x[3][-1], cot_seen[0])
    y[4] = turn_over(4, x[4], y[2][1][-1], cot_seen[1])
    y[5] = turn_over(5, x[5], y[3][1][-1], x[4][-1])
    if shifted:
        tok = call(
            join_kernel,
            shape(rows, half, BF16),
            tok,
            [ANY] * blocks,
            [pltpu.SemaphoreType.DMA((blocks,))],
            outs=ANY,
            moved=4 * rows * half,
        )
    else:
        tok = tok[0]
    other_tok = shift(tok, "tensor", 1)

    def held_by(picked):
        return [k for i in picked for k in y[i][0]], [p for i in picked for p in y[i][1]]

    gate_keys, gate_pieces = held_by([0, 1])
    up_keys, up_pieces = held_by([2, 3])
    down_keys, down_pieces = held_by([4, 5])

    def front(own, keys, pieces, gate, *held):
        final = gate is not None
        act = shape(rows, wide, F32)
        return call(
            functools.partial(front_kernel, sizes, keys, final),
            [act, shape(rows, wide, BF16)] if final else [act],
            (where, tok, other_tok, own, *pieces, *([gate] if final else []), *held),
            [SMEM] + [ANY] * (3 + len(pieces)) + [VMEM] * final + [ANY] * len(held),
            [
                pltpu.VMEM((rows, feats), BF16),
                pltpu.VMEM((wide, feats), BF16),
                pltpu.SemaphoreType.DMA((3 + len(pieces),)),
            ],
            flops=2 * rows * feats * units,
            moved=2 * feats * (rows + units),
        )

    (gate,) = front(gate_t, gate_keys, gate_pieces, None)
    up, hidden = front(up_t, up_keys, up_pieces, gate, cot_seen[1])
    other_hidden = shift(hidden, "tensor", 1)

    width = half // n_groups // COL_CHUNKS
    back = []
    for part in range(COL_CHUNKS):
        picked = [i for i, key in enumerate(down_keys) if key[0] == part]
        held = [b[0] for b in back]
        outs = call(
            functools.partial(out_kernel, sizes, [down_keys[i] for i in picked], part, blocks),
            [shape(each, n_groups * width, BF16)] * blocks,
            (where, hidden, other_hidden, down, *[down_pieces[i] for i in picked], cot_seen[2], *held),
            [SMEM] + [ANY] * (4 + len(picked) + len(held)),
            [
                pltpu.VMEM((rows, 2 * wide), BF16),
                pltpu.VMEM((2 * wide, n_groups * width), BF16),
                pltpu.SemaphoreType.DMA((2 + n_groups + len(picked),)),
            ],
            flops=4 * rows * units * n_groups * width,
            moved=4 * units * n_groups * width,
        )
        back.append(travel(outs, -1, back[-1] if back else ()))

    kept, sent = call(
        functools.partial(cot_kernel, sizes, down_keys, blocks),
        [shape(rows, wide, F32), shape(rows, wide, BF16)],
        (where, *cot, down, *down_pieces, back[-1][0]),
        [SMEM] + [ANY] * (blocks + 2 + len(down_pieces)),
        [
            pltpu.VMEM((rows, half), BF16),
            pltpu.VMEM((2 * wide, half), BF16),
            pltpu.SemaphoreType.DMA((COL_CHUNKS * n_groups * (blocks + 1) + len(down_pieces),)),
        ],
        flops=4 * rows * half * units,
        moved=4 * half * units,
    )
    received = shift(sent, "tensor", 1)
    kept, sent = call(
        functools.partial(grad_kernel, sizes, gate_keys, up_keys),
        [shape(rows, half, F32), shape(rows, half, BF16)],
        (where, gate, up, kept, received, gate_t, up_t, *gate_pieces, *up_pieces, *[back[0][s] for s in order[:2] if shifted]),
        [SMEM] + [VMEM] * 4 + [ANY] * (2 + len(gate_pieces) + len(up_pieces) + 2 * shifted),
        [
            pltpu.VMEM((wide, feats), BF16),
            pltpu.VMEM((wide, feats), BF16),
            pltpu.SemaphoreType.DMA((2 + len(gate_pieces) + len(up_pieces),)),
        ],
        flops=4 * rows * feats * units,
        moved=4 * feats * units,
    )
    received = shift(sent, "tensor", 1)
    slots = call(add_kernel, [shape(each, half, BF16)] * blocks, (kept, received), [VMEM] * 2, moved=8 * rows * half)
    grad_back = travel(slots, -1, back[-1])

    layer_out, prob_part, both = call(
        functools.partial(layer_kernel, experts, cap, blocks, n_groups),
        [shape(count, half, BF16), shape(expert_ids.shape[1], count, F32), shape(count, rows, BF16)],
        (where, expert_ids.T, gate_probs.T, cotangent, *[part for parts in back for part in parts]),
        [SMEM] + [VMEM] * (3 + COL_CHUNKS * blocks),
        flops=4 * count * rows * half,
        moved=2 * rows * half,
    )
    grad_probs = (prob_part + shift(prob_part, "tensor", 1)).T
    (grad_tokens,) = call(
        token_kernel,
        [shape(count, half, BF16)],
        (both, *grad_back),
        [VMEM] * (1 + blocks),
        flops=2 * count * rows * half,
        moved=2 * rows * half,
    )
    return (layer_out, grad_tokens, grad_probs)


def solution(mesh):
    by_token = ("groups", "expert", "dp")
    weight = P("expert", "dp", "tensor")
    in_specs = (P(by_token, "tensor"), P(by_token, "tensor"), P(by_token, None), P(by_token, None)) + (weight,) * 3
    out_specs = (P(by_token, "tensor"), P(by_token, "tensor"), P(by_token, None))
    return jax.shard_map(local, mesh=mesh, in_specs=in_specs, out_specs=out_specs, check_vma=False)
```

```python
import functools

import jax
import jax.numpy as jnp
from jax import lax
from jax.experimental import pallas as pl
from jax.experimental.pallas import tpu as pltpu
from jax.sharding import PartitionSpec as P

F32 = jnp.float32
BF16 = jnp.bfloat16
LAST = (((1,), (1,)), ((), ()))
ROW_CHUNKS = 2
COL_CHUNKS = 2
SHIFTED_UP_TO = 8

VMEM = pl.BlockSpec(memory_space=pltpu.VMEM)
ANY = pl.BlockSpec(memory_space=pl.ANY)


def dot(a, b, dims=(((1,), (0,)), ((), ()))):
    return lax.dot_general(a, b, dims, preferred_element_type=F32)


def call(kernel, out_shape, args, held=(), scratch=(), flops=0, moved=0):
    several = isinstance(out_shape, list)
    given = len(args)

    def body(*refs):
        kernel(*refs[:given], *refs[given + len(held) :])

    return pl.pallas_call(
        body,
        out_shape=out_shape,
        in_specs=[VMEM] * given + [ANY] * len(held),
        out_specs=[VMEM] * len(out_shape) if several else VMEM,
        scratch_shapes=list(scratch),
        compiler_params=pltpu.CompilerParams(vmem_limit_bytes=24 * 1024 * 1024),
        cost_estimate=pl.CostEstimate(flops=flops, bytes_accessed=moved, transcendentals=0),
    )(*args, *held)


def shape(rows, cols, dtype):
    return jax.ShapeDtypeStruct((rows, cols), dtype)


def padded(size):
    return -(-size // 128) * 128


def before(index, step, size):
    moved = index - step
    return jnp.where(moved < 0, moved + size, moved)


def rows_at(start, size):
    return pl.ds(pl.multiple_of(start, 16), size)


def cols_at(start, size):
    return pl.ds(pl.multiple_of(start, 128), size)


def places(experts, cap, rotated, start, size, ids_t):
    count = ids_t.shape[1]
    row = lax.broadcasted_iota(jnp.int32, (size, 1), 0) + start
    block = jnp.zeros_like(row)
    for later in range(1, experts):
        block = block + (row >= later * cap).astype(jnp.int32)
    expert = block + (lax.axis_index("expert") if rotated else 0)
    expert = jnp.where(expert >= experts, expert - experts, expert)
    slot = (row - block * cap).astype(F32)
    first = ids_t[0:1, :] == expert
    second = ids_t[1:2, :] == expert
    before_it = lax.broadcasted_iota(jnp.int32, (count, count), 0) < lax.broadcasted_iota(jnp.int32, (count, count), 1)
    earlier = dot((first | second).astype(F32).astype(BF16), before_it.astype(F32).astype(BF16))
    here = earlier == slot
    return first & here, second & here


def token_rows_kernel(experts, cap, rotated, ids_t, tok, *outs):
    each = outs[0].shape[0]
    first, second = places(experts, cap, rotated, 0, each * len(outs), ids_t)
    rows = dot((first | second).astype(F32).astype(BF16), tok[...]).astype(BF16)
    for i, out in enumerate(outs):
        out[...] = rows[i * each : (i + 1) * each]


def cot_rows_kernel(experts, cap, rotated, blocks, ids_t, probs_t, cot, *outs):
    each = outs[0].shape[0]
    for block, out in zip(blocks, outs):
        first, second = places(experts, cap, rotated, block * each, each, ids_t)
        weight = jnp.where(first, probs_t[0:1, :], jnp.where(second, probs_t[1:2, :], 0.0))
        weight = jnp.sum(weight, axis=1, keepdims=True)
        rows = dot((first | second).astype(F32).astype(BF16), cot[...])
        out[...] = (weight * rows).astype(BF16)


def cut_kernel(axis, chunk, n_groups, weight, out):
    size = out.shape[axis]
    start = lax.axis_index("groups") * (weight.shape[axis] // n_groups) + chunk * size
    out[...] = weight[rows_at(start, size), :] if axis == 0 else weight[:, cols_at(start, size)]


def join_kernel(*refs):
    at = 0
    for part in refs[:-1]:
        refs[-1][pl.ds(at, part.shape[0]), :] = part[...]
        at += part.shape[0]


def fill_wide(sizes, own, pieces, dst):
    n_dp, n_groups = sizes
    units, feats = own.shape
    group, place = lax.axis_index("groups"), lax.axis_index("dp")
    dst[pl.ds(0, units), cols_at(place * feats, feats)] = own[...]
    share = units // n_groups
    for (chunk, step, turn), ref in pieces:
        start = before(group, turn, n_groups) * share + chunk * ref.shape[0]
        dst[rows_at(start, ref.shape[0]), cols_at(before(place, step, n_dp) * feats, feats)] = ref[...]
    if dst.shape[0] > units:
        dst[units:, :] = jnp.zeros((dst.shape[0] - units, dst.shape[1]), dst.dtype)


def fill_down(sizes, part, own, pieces, dst):
    n_dp, n_groups = sizes
    units, feats = own.shape
    half = dst.shape[0] // 2
    per_half = n_dp // 2
    share = feats // n_groups
    width = share // COL_CHUNKS
    group, place = lax.axis_index("groups"), lax.axis_index("dp")

    def start(index):
        upper = (index >= per_half).astype(jnp.int32)
        return upper * half + (index - upper * per_half) * units

    for g in range(n_groups):
        dst[rows_at(start(place), units), pl.ds(g * width, width)] = own[:, pl.ds(g * share + part * width, width)]
    for (_, step, turn), ref in pieces:
        cols = cols_at(before(group, turn, n_groups) * width, width)
        dst[rows_at(start(before(place, step, n_dp)), units), cols] = ref[...]
    used = per_half * units
    if half > used:
        for side in range(2):
            dst[side * half + used : (side + 1) * half, :] = jnp.zeros((half - used, dst.shape[1]), dst.dtype)


def halves(size):
    core = lax.axis_index("tensor")
    return core * size, (1 - core) * size


def front_kernel(sizes, keys, final, own_tok, other_tok, own, *refs):
    pieces, refs = list(zip(keys, refs[: len(keys)])), refs[len(keys) :]
    weight, act_out = refs[-2:]
    fill_wide(sizes, own, pieces, weight)
    half = own_tok.shape[1]
    mine, theirs = halves(half)
    value = dot(own_tok[...], weight[:, cols_at(mine, half)], LAST) + dot(other_tok[...], weight[:, cols_at(theirs, half)], LAST)
    act_out[...] = value
    if final:
        gate, hidden_out = refs[:2]
        hidden_out[...] = (gate[...] * jax.nn.sigmoid(gate[...]) * value).astype(BF16)


def out_kernel(sizes, keys, part, own_hidden, other_hidden, own, *refs):
    pieces, (weight, *outs) = list(zip(keys, refs[: len(keys)])), refs[len(keys) :]
    fill_down(sizes, part, own, pieces, weight)
    half = own_hidden.shape[1]
    mine, theirs = halves(half)
    value = dot(own_hidden[...], weight[rows_at(mine, half), :]) + dot(other_hidden[...], weight[rows_at(theirs, half), :])
    value = value.astype(BF16)
    each = outs[0].shape[0]
    for i, out in enumerate(outs):
        out[...] = value[i * each : (i + 1) * each]


def cot_kernel(n_groups, cots, *refs):
    weights, (send, keep) = refs[:-2], refs[-2:]
    half = send.shape[1]
    share = cots.shape[1] // n_groups
    width = share // COL_CHUNKS
    mine, theirs = halves(half)
    for start, out in ((theirs, send), (mine, keep)):
        total = 0.0
        for part, weight in enumerate(weights):
            for g in range(n_groups):
                rows = cots[:, pl.ds(g * share + part * width, width)]
                total = total + dot(rows, weight[rows_at(start, half), pl.ds(g * width, width)], LAST)
        out[...] = total.astype(out.dtype)


def grad_kernel(gate, up, kept, received, w_gate, w_up, send, keep):
    gate_act = gate[...]
    sigmoid_g = jax.nn.sigmoid(gate_act)
    hidden_grad = kept[...] + received[...].astype(F32)
    gate_grad = (hidden_grad * up[...] * sigmoid_g * (1.0 + gate_act * (1.0 - sigmoid_g))).astype(BF16)
    up_grad = (hidden_grad * gate_act * sigmoid_g).astype(BF16)
    half = keep.shape[1]
    mine, theirs = halves(half)
    for start, out in ((theirs, send), (mine, keep)):
        cols = cols_at(start, half)
        out[...] = (dot(gate_grad, w_gate[:, cols]) + dot(up_grad, w_up[:, cols])).astype(out.dtype)


def add_kernel(kept, received, *outs):
    value = (kept[...] + received[...].astype(F32)).astype(BF16)
    each = outs[0].shape[0]
    for i, out in enumerate(outs):
        out[...] = value[i * each : (i + 1) * each]


def layer_kernel(experts, cap, rotated, n_groups, part, ids_t, probs_t, cot, *refs):
    back, (out, prob_out, both_out) = refs[:-3], refs[-3:]
    share = cot.shape[1] // n_groups
    width = share // COL_CHUNKS
    back = jnp.concatenate([r[...] for r in back], axis=0)
    first, second = (m.astype(F32).T.astype(BF16) for m in places(experts, cap, rotated, 0, back.shape[0], ids_t))
    both_out[...] = first + second
    probs = jnp.concatenate([probs_t[...], jnp.zeros((6, probs_t.shape[1]), F32)], axis=0).T
    slots = dot(first, back), dot(second, back)
    out[...] = (probs[:, 0:1] * slots[0] + probs[:, 1:2] * slots[1]).astype(BF16)
    sums = [0.0, 0.0]
    for g in range(n_groups):
        cot_here = cot[:, pl.ds(g * share + part * width, width)].astype(F32)
        for k in range(2):
            sums[k] = sums[k] + jnp.sum(slots[k][:, g * width : (g + 1) * width] * cot_here, axis=1, keepdims=True)
    lane = lax.broadcasted_iota(jnp.int32, (cot.shape[0], 128), 1)
    prob_out[...] = jnp.where(lane == 0, sums[0], sums[1]).T[0:2, :]


def token_kernel(n_groups, both, *refs):
    back, layers, (grad_out, layer_out) = refs[: -2 - COL_CHUNKS], refs[-2 - COL_CHUNKS : -2], refs[-2:]
    width = layers[0].shape[1] // n_groups
    for part, layer in enumerate(layers):
        for g in range(n_groups):
            layer_out[:, pl.ds((g * COL_CHUNKS + part) * width, width)] = layer[:, pl.ds(g * width, width)]
    grad_out[...] = dot(both[...], jnp.concatenate([r[...] for r in back], axis=0)).astype(BF16)


def shift(value, axis, step):
    size = lax.axis_size(axis)
    return lax.ppermute(value, axis, [(i, (i + step) % size) for i in range(size)])


def local(tokens, cotangent, expert_ids, gate_probs, w_gate, w_up, w_down):
    count, half = tokens.shape
    experts, n_dp, n_groups = lax.axis_size("expert"), lax.axis_size("dp"), lax.axis_size("groups")
    sizes = (n_dp, n_groups)
    cap = 3 * count * expert_ids.shape[1] // (2 * experts)
    rows = experts * cap
    shifted = experts <= SHIFTED_UP_TO
    blocks = experts if shifted else 1
    each = rows // blocks
    routing = (experts, cap, shifted)
    order = [experts // 2] + [s for s in range(1, experts) if s != experts // 2]

    def travel(part, sign, s):
        if shifted:
            return shift(part, "expert", sign * s) if s else part
        part = lax.all_to_all(part.reshape(experts, cap, -1), "expert", split_axis=0, concat_axis=0, tiled=True)
        return part.reshape(rows, -1)

    gate_t, up_t, down = jnp.swapaxes(w_gate[0], 0, 1), jnp.swapaxes(w_up[0], 0, 1), w_down[0]
    ids_t, probs_t = expert_ids.T, gate_probs.T
    units = gate_t.shape[0]
    wide = padded(units)
    feats = n_dp * gate_t.shape[1]
    plan = [(gate_t, 0, c) for c in range(ROW_CHUNKS)] + [(up_t, 0, c) for c in range(ROW_CHUNKS)]
    plan += [(down, 1, c) for c in range(COL_CHUNKS)]
    x, y, cuts = {}, {}, []

    def cut(i, *held):
        weight, axis, chunk = plan[i]
        size = weight.shape[axis] // n_groups // (COL_CHUNKS if axis else ROW_CHUNKS)
        mine = call(
            functools.partial(cut_kernel, axis, chunk, n_groups),
            shape(weight.shape[0] if axis else size, size if axis else weight.shape[1], BF16),
            (weight,),
            (*held, *cuts[-1:]),
        )
        cuts.append(mine)
        x[i] = [shift(mine, "dp", step) for step in range(1, n_dp)]

    def turn_over(i):
        y[i] = []
        for step, here in enumerate(x[i], 1):
            for turn in range(n_groups):
                y[i].append(((plan[i][2], step, turn), shift(here, "groups", turn) if turn else here))

    cut(0)
    tok_send = call(
        functools.partial(token_rows_kernel, *routing),
        [shape(each, half, BF16)] * blocks,
        (ids_t, tokens),
        cuts[-1:],
        flops=2 * rows * count * half,
        moved=2 * (count + rows) * half,
    )
    cut(1)

    def send_cot(picked, *held):
        made = call(
            functools.partial(cot_rows_kernel, *routing, picked),
            [shape(each, half, BF16)] * len(picked),
            (ids_t, probs_t, cotangent),
            held,
            flops=2 * each * len(picked) * count * half,
            moved=2 * (count + each * len(picked)) * half,
        )
        return [travel(part, 1, s) for part, s in zip(made, picked)]

    tok = [travel(part, 1, s) for s, part in enumerate(tok_send)]
    turn_over(0)
    turn_over(1)
    if shifted:
        t = [tok[s] for s in order]
        cut(2, x[0][-1])
        cut(3, x[1][-1], t[0], t[1])
        cot = dict(zip((0, order[0]), send_cot((0, order[0]), *t[:-1], x[1][-1])))
        cut(4, x[2][-1], *t)
        for i in range(1, len(order)):
            (cot[order[i]],) = send_cot((order[i],), cot[order[i - 1]], *t)
        cut(5, x[3][-1], cot[order[0]])
        cot_parts = [cot[s] for s in range(blocks)]
        tok_all = call(join_kernel, shape(rows, half, BF16), tok)
    else:
        cut(2, x[0][-1])
        cut(3, x[1][-1])
        cut(4, x[2][-1])
        cut(5, x[3][-1])
        cot_parts = send_cot((0,))
        (tok_all,) = tok
    for i in range(2, len(plan)):
        turn_over(i)
    other_tok = shift(tok_all, "tensor", 1)

    def front(own, picked, gate, *held):
        final = gate is not None
        keys, pieces = zip(*[kp for i in picked for kp in y[i]])
        act = shape(rows, wide, F32)
        return call(
            functools.partial(front_kernel, sizes, keys, final),
            ([shape(rows, wide, BF16)] if final else []) + [shape(wide, feats, BF16), act],
            (tok_all, other_tok, own, *pieces, *([gate] if final else [])),
            held,
            flops=2 * rows * feats * units,
            moved=2 * feats * (rows + units),
        )

    first_pieces = range(ROW_CHUNKS)
    gate_weight, gate = front(gate_t, list(first_pieces), None)
    hidden, up_weight, up = front(up_t, [ROW_CHUNKS + i for i in first_pieces], gate, *cot_parts[1:2])
    other_hidden = shift(hidden, "tensor", 1)
    cot_all = call(join_kernel, shape(rows, half, BF16), cot_parts) if shifted else cot_parts[0]

    width = half // n_groups // COL_CHUNKS
    down_weights, layers, sent, prob_part = [], [], [], 0.0
    made = ()
    for part in range(COL_CHUNKS):
        keys, pieces = zip(*y[2 * ROW_CHUNKS + part])
        weight, *made = call(
            functools.partial(out_kernel, sizes, keys, part),
            [shape(2 * wide, n_groups * width, BF16)] + [shape(each, n_groups * width, BF16)] * blocks,
            (hidden, other_hidden, down, *pieces),
            made[:1],
            flops=4 * rows * units * n_groups * width,
            moved=4 * units * n_groups * width,
        )
        down_weights.append(weight)
        back = [travel(out, -1, s) for s, out in enumerate(made)]
        sent.append(back)
        layer, prob, both = call(
            functools.partial(layer_kernel, *routing, n_groups, part),
            [shape(count, n_groups * width, BF16), shape(expert_ids.shape[1], count, F32), shape(count, rows, BF16)],
            (ids_t, probs_t, cotangent, *back),
            flops=4 * count * rows * n_groups * width,
            moved=2 * rows * n_groups * width,
        )
        layers.append(layer)
        prob_part = prob_part + prob

    crossing, kept = call(
        functools.partial(cot_kernel, n_groups),
        [shape(rows, wide, BF16), shape(rows, wide, F32)],
        (cot_all, *down_weights),
        made[:1],
        flops=4 * rows * half * units,
        moved=4 * half * units,
    )
    received = shift(crossing, "tensor", 1)
    crossing, kept = call(
        grad_kernel,
        [shape(rows, half, BF16), shape(rows, half, F32)],
        (gate, up, kept, received, gate_weight, up_weight),
        layers[:1],
        flops=4 * rows * feats * units,
        moved=4 * feats * units,
    )
    received = shift(crossing, "tensor", 1)
    slots = call(add_kernel, [shape(each, half, BF16)] * blocks, (kept, received), sent[-1][1:3], moved=8 * rows * half)
    grad_back = [travel(part, -1, s) for s, part in enumerate(slots)]
    grad_probs = (prob_part + shift(prob_part, "tensor", 1)).T
    grad_tokens, layer_out = call(
        functools.partial(token_kernel, n_groups),
        [shape(count, half, BF16)] * 2,
        (both, *grad_back, *layers),
        flops=2 * count * rows * half,
        moved=2 * rows * half,
    )
    return (layer_out, grad_tokens, grad_probs)


def solution(mesh):
    by_token = ("groups", "expert", "dp")
    weight = P("expert", "dp", "tensor")
    in_specs = (P(by_token, "tensor"), P(by_token, "tensor"), P(by_token, None), P(by_token, None)) + (weight,) * 3
    out_specs = (P(by_token, "tensor"), P(by_token, "tensor"), P(by_token, None))
    return jax.shard_map(local, mesh=mesh, in_specs=in_specs, out_specs=out_specs, check_vma=False)
```

```python
import functools

import jax
import jax.numpy as jnp
from jax import lax
from jax.experimental import pallas as pl
from jax.experimental.pallas import tpu as pltpu
from jax.sharding import PartitionSpec as P

F32 = jnp.float32
BF16 = jnp.bfloat16
LAST = (((1,), (1,)), ((), ()))
ROW_CHUNKS = 2
COL_CHUNKS = 2
SWAPS = 4
SHIFTED_UP_TO = 8

VMEM = pl.BlockSpec(memory_space=pltpu.VMEM)
ANY = pl.BlockSpec(memory_space=pl.ANY)


def dot(a, b, dims=(((1,), (0,)), ((), ()))):
    return lax.dot_general(a, b, dims, preferred_element_type=F32)


def call(kernel, out_shape, args, held=(), scratch=()):
    several = isinstance(out_shape, list)
    given = len(args)

    def body(*refs):
        kernel(*refs[:given], *refs[given + len(held) :])

    return pl.pallas_call(
        body,
        out_shape=out_shape,
        in_specs=[VMEM] * given + [ANY] * len(held),
        out_specs=[VMEM] * len(out_shape) if several else VMEM,
        scratch_shapes=list(scratch),
        compiler_params=pltpu.CompilerParams(vmem_limit_bytes=24 * 1024 * 1024),
        cost_estimate=pl.CostEstimate(flops=1, bytes_accessed=1, transcendentals=0),
    )(*args, *held)


def shape(rows, cols, dtype):
    return jax.ShapeDtypeStruct((rows, cols), dtype)


def made_shape(value):
    return shape(*value.shape, value.dtype)


def padded(size):
    return -(-size // 128) * 128


def before(index, step, size):
    moved = index - step
    return jnp.where(moved < 0, moved + size, moved)


def rows_at(start, size):
    return pl.ds(pl.multiple_of(start, 16), size)


def cols_at(start, size):
    return pl.ds(pl.multiple_of(start, 128), size)


def places(experts, cap, rotated, start, size, ids_t):
    count = ids_t.shape[1]
    row = lax.broadcasted_iota(jnp.int32, (size, 1), 0) + start
    block = jnp.zeros_like(row)
    for later in range(1, experts):
        block = block + (row >= later * cap).astype(jnp.int32)
    expert = block + (lax.axis_index("expert") if rotated else 0)
    expert = jnp.where(expert >= experts, expert - experts, expert)
    slot = (row - block * cap).astype(F32)
    first = ids_t[0:1, :] == expert
    second = ids_t[1:2, :] == expert
    before_it = lax.broadcasted_iota(jnp.int32, (count, count), 0) < lax.broadcasted_iota(jnp.int32, (count, count), 1)
    earlier = dot((first | second).astype(F32).astype(BF16), before_it.astype(F32).astype(BF16))
    here = earlier == slot
    return first & here, second & here


def token_rows_kernel(experts, cap, rotated, blocks, ids_t, tok, *outs):
    each = outs[0].shape[0]
    for block, out in zip(blocks, outs):
        first, second = places(experts, cap, rotated, block * each, each, ids_t)
        out[...] = dot((first | second).astype(F32).astype(BF16), tok[...]).astype(BF16)


def cot_rows_kernel(experts, cap, rotated, blocks, ids_t, probs_t, cot, *outs):
    each = outs[0].shape[0]
    for block, out in zip(blocks, outs):
        first, second = places(experts, cap, rotated, block * each, each, ids_t)
        weight = jnp.where(first, probs_t[0:1, :], jnp.where(second, probs_t[1:2, :], 0.0))
        weight = jnp.sum(weight, axis=1, keepdims=True)
        rows = dot((first | second).astype(F32).astype(BF16), cot[...])
        out[...] = (weight * rows).astype(BF16)


def cut_kernel(axis, chunk, n_groups, weight, out):
    size = out.shape[axis]
    start = lax.axis_index("groups") * (weight.shape[axis] // n_groups) + chunk * size
    out[...] = weight[rows_at(start, size), :] if axis == 0 else weight[:, cols_at(start, size)]


def join_kernel(*refs):
    at = 0
    for part in refs[:-1]:
        refs[-1][pl.ds(at, part.shape[0]), :] = part[...]
        at += part.shape[0]


def fill_wide(sizes, own, pieces, dst):
    n_dp, n_groups = sizes
    units, feats = own.shape
    group, place = lax.axis_index("groups"), lax.axis_index("dp")
    dst[pl.ds(0, units), cols_at(place * feats, feats)] = own[...]
    share = units // n_groups
    for (chunk, step, turn), ref in pieces:
        start = before(group, turn, n_groups) * share + chunk * ref.shape[0]
        dst[rows_at(start, ref.shape[0]), cols_at(before(place, step, n_dp) * feats, feats)] = ref[...]
    if dst.shape[0] > units:
        dst[units:, :] = jnp.zeros((dst.shape[0] - units, dst.shape[1]), dst.dtype)


def fill_down(sizes, part, own, pieces, dst):
    n_dp, n_groups = sizes
    units, feats = own.shape
    half = dst.shape[0] // 2
    per_half = n_dp // 2
    share = feats // n_groups
    width = share // COL_CHUNKS
    group, place = lax.axis_index("groups"), lax.axis_index("dp")

    def start(index):
        upper = (index >= per_half).astype(jnp.int32)
        return upper * half + (index - upper * per_half) * units

    for g in range(n_groups):
        dst[rows_at(start(place), units), pl.ds(g * width, width)] = own[:, pl.ds(g * share + part * width, width)]
    for (_, step, turn), ref in pieces:
        cols = cols_at(before(group, turn, n_groups) * width, width)
        dst[rows_at(start(before(place, step, n_dp)), units), cols] = ref[...]
    used = per_half * units
    if half > used:
        for side in range(2):
            dst[side * half + used : (side + 1) * half, :] = jnp.zeros((half - used, dst.shape[1]), dst.dtype)


def put_rows(value, outs):
    each = outs[0].shape[0]
    for i, out in enumerate(outs):
        out[...] = value[i * each : (i + 1) * each].astype(out.dtype)


def halves(size):
    core = lax.axis_index("tensor")
    return core * size, (1 - core) * size


def front_kernel(sizes, keys, final, own_tok, other_tok, own, *refs):
    pieces, refs = list(zip(keys, refs[: len(keys)])), refs[len(keys) :]
    weight, act_out = refs[:2] if not final else refs[1:3]
    fill_wide(sizes, own, pieces, weight)
    half = own_tok.shape[1]
    mine, theirs = halves(half)
    value = dot(own_tok[...], weight[:, cols_at(mine, half)], LAST) + dot(other_tok[...], weight[:, cols_at(theirs, half)], LAST)
    act_out[...] = value
    if final:
        gate, hidden_out = refs[0], refs[3:]
        hidden = (gate[...] * jax.nn.sigmoid(gate[...]) * value).astype(BF16)
        put_rows(hidden, hidden_out)


def out_kernel(sizes, keys, part, own_hidden, other_hidden, own, *refs):
    pieces, (weight, *outs) = list(zip(keys, refs[: len(keys)])), refs[len(keys) :]
    fill_down(sizes, part, own, pieces, weight)
    half = own_hidden.shape[1]
    mine, theirs = halves(half)
    value = dot(own_hidden[...], weight[rows_at(mine, half), :]) + dot(other_hidden[...], weight[rows_at(theirs, half), :])
    put_rows(value, outs)


def cot_kernel(n_groups, cots, *refs):
    weights, keep, send = refs[:COL_CHUNKS], refs[COL_CHUNKS], refs[COL_CHUNKS + 1 :]
    half = keep.shape[1]
    share = cots.shape[1] // n_groups
    width = share // COL_CHUNKS
    mine, theirs = halves(half)
    for start, outs in ((theirs, send), (mine, [keep])):
        total = 0.0
        for part, weight in enumerate(weights):
            for g in range(n_groups):
                rows = cots[:, pl.ds(g * share + part * width, width)]
                total = total + dot(rows, weight[rows_at(start, half), pl.ds(g * width, width)], LAST)
        put_rows(total, outs)


def grad_kernel(gate, up, kept, received, w_gate, w_up, keep, *send):
    gate_act = gate[...]
    sigmoid_g = jax.nn.sigmoid(gate_act)
    hidden_grad = kept[...] + received[...].astype(F32)
    gate_grad = (hidden_grad * up[...] * sigmoid_g * (1.0 + gate_act * (1.0 - sigmoid_g))).astype(BF16)
    up_grad = (hidden_grad * gate_act * sigmoid_g).astype(BF16)
    half = keep.shape[1]
    mine, theirs = halves(half)
    for start, outs in ((theirs, send), (mine, [keep])):
        cols = cols_at(start, half)
        put_rows(dot(gate_grad, w_gate[:, cols]) + dot(up_grad, w_up[:, cols]), outs)


def add_kernel(kept, received, *outs):
    put_rows(kept[...] + received[...].astype(F32), outs)


def layer_kernel(experts, cap, rotated, n_groups, part, ids_t, probs_t, cot, *refs):
    back, (out, prob_out, both_out) = refs[:-3], refs[-3:]
    share = cot.shape[1] // n_groups
    width = share // COL_CHUNKS
    back = jnp.concatenate([r[...] for r in back], axis=0)
    first, second = (m.astype(F32).T.astype(BF16) for m in places(experts, cap, rotated, 0, back.shape[0], ids_t))
    both_out[...] = first + second
    probs = jnp.concatenate([probs_t[...], jnp.zeros((6, probs_t.shape[1]), F32)], axis=0).T
    slots = dot(first, back), dot(second, back)
    out[...] = (probs[:, 0:1] * slots[0] + probs[:, 1:2] * slots[1]).astype(BF16)
    sums = [0.0, 0.0]
    for g in range(n_groups):
        cot_here = cot[:, pl.ds(g * share + part * width, width)].astype(F32)
        for k in range(2):
            sums[k] = sums[k] + jnp.sum(slots[k][:, g * width : (g + 1) * width] * cot_here, axis=1, keepdims=True)
    lane = lax.broadcasted_iota(jnp.int32, (cot.shape[0], 128), 1)
    prob_out[...] = jnp.where(lane == 0, sums[0], sums[1]).T[0:2, :]


def token_kernel(n_groups, both, *refs):
    back, layers, (grad_out, layer_out) = refs[: -2 - COL_CHUNKS], refs[-2 - COL_CHUNKS : -2], refs[-2:]
    width = layers[0].shape[1] // n_groups
    for part, layer in enumerate(layers):
        for g in range(n_groups):
            layer_out[:, pl.ds((g * COL_CHUNKS + part) * width, width)] = layer[:, pl.ds(g * width, width)]
    grad_out[...] = dot(both[...], jnp.concatenate([r[...] for r in back], axis=0)).astype(BF16)


def shift(value, axis, step):
    size = lax.axis_size(axis)
    return lax.ppermute(value, axis, [(i, (i + step) % size) for i in range(size)])


def swapped(parts):
    return [shift(part, "tensor", 1) for part in parts]


def joined(parts):
    if len(parts) == 1:
        return parts[0]
    return call(join_kernel, shape(sum(p.shape[0] for p in parts), parts[0].shape[1], parts[0].dtype), parts)


def local(tokens, cotangent, expert_ids, gate_probs, w_gate, w_up, w_down):
    count, half = tokens.shape
    experts, n_dp, n_groups = lax.axis_size("expert"), lax.axis_size("dp"), lax.axis_size("groups")
    sizes = (n_dp, n_groups)
    cap = 3 * count * expert_ids.shape[1] // (2 * experts)
    rows = experts * cap
    shifted = experts <= SHIFTED_UP_TO
    blocks = experts if shifted else 1
    each = rows // blocks
    routing = (experts, cap, shifted)
    order = [s for s in range(1, experts) if s != experts // 2] + [experts // 2]

    def travel(part, sign, s):
        if shifted:
            return shift(part, "expert", sign * s) if s else part
        part = lax.all_to_all(part.reshape(experts, cap, -1), "expert", split_axis=0, concat_axis=0, tiled=True)
        return part.reshape(rows, -1)

    gate_t, up_t, down = jnp.swapaxes(w_gate[0], 0, 1), jnp.swapaxes(w_up[0], 0, 1), w_down[0]
    ids_t, probs_t = expert_ids.T, gate_probs.T
    units = gate_t.shape[0]
    wide = padded(units)
    feats = n_dp * gate_t.shape[1]
    plan = [(gate_t, 0, c) for c in range(ROW_CHUNKS)] + [(up_t, 0, c) for c in range(ROW_CHUNKS)]
    plan += [(down, 1, c) for c in range(COL_CHUNKS)]
    x, y, cuts = {}, {}, []

    def cut(i, *held):
        weight, axis, chunk = plan[i]
        size = weight.shape[axis] // n_groups // (COL_CHUNKS if axis else ROW_CHUNKS)
        mine = call(
            functools.partial(cut_kernel, axis, chunk, n_groups),
            shape(weight.shape[0] if axis else size, size if axis else weight.shape[1], BF16),
            (weight,),
            (*held, *cuts[-1:]),
        )
        cuts.append(mine)
        x[i] = [shift(mine, "dp", step) for step in range(1, n_dp)]

    def turn_over(i, *held):
        y[i] = []
        for step, here in enumerate(x[i], 1):
            on = call(join_kernel, made_shape(here), (here,), held)
            for turn in range(n_groups):
                y[i].append(((plan[i][2], step, turn), shift(on, "groups", turn) if turn else here))

    cut(0)
    cut(1)

    def send(kernel, args, picked, *held):
        made = call(
            functools.partial(kernel, *routing, picked),
            [shape(each, half, BF16)] * len(picked),
            args,
            held,
        )
        return [travel(part, 1, s) for part, s in zip(made, picked)]

    send_tok = functools.partial(send, token_rows_kernel, (ids_t, tokens))
    send_cot = functools.partial(send, cot_rows_kernel, (ids_t, probs_t, cotangent))
    last = [()] * len(plan)
    cot_parts = []
    if shifted:
        tok, cot, now = {}, {}, ()
        for i, (made, blocks_in, name) in enumerate([(tok, send_tok, s) for s in order] + [(cot, send_cot, s) for s in order]):
            picked = (name,) if name != order[0] else (0, name)
            waits = [*now, x[i - 1][-1]] if 0 < i <= len(plan) else list(now)
            if i:
                turn_over(i - 1, *(y[i - 3][-1][1:] if i >= 3 else ()), *last[i - 1])
                if i + 1 < len(plan):
                    cut(i + 1, x[i - 1][-1], *(y[i - 2][-1][1:] if i >= 2 else ()))
            made.update(zip(picked, blocks_in(picked, *waits, *(cuts[:1] if i == 0 else ()))))
            now = (made[name],)
            if i + 1 < len(plan):
                last[i + 1] = now
        turn_over(5, y[3][-1][1], *now)
        cot_parts = [cot[s] for s in range(blocks)]
        tok_parts = [tok[s] for s in range(blocks)]
    else:
        for i in range(len(plan)):
            if i > 1:
                cut(i, x[i - 2][-1])
            turn_over(i)
        cot_parts = send_cot((0,))
        tok_parts = send_tok((0,))
    tok_all, other_tok = joined(tok_parts), joined(swapped(tok_parts))

    def front(own, picked, gate, *held):
        final = gate is not None
        keys, pieces = zip(*[kp for i in picked for kp in y[i]])
        act = shape(rows, wide, F32)
        return call(
            functools.partial(front_kernel, sizes, keys, final),
            [shape(wide, feats, BF16), act] + ([shape(rows // SWAPS, wide, BF16)] * SWAPS if final else []),
            (tok_all, other_tok, own, *pieces, *([gate] if final else [])),
            held,
        )

    first_pieces = range(ROW_CHUNKS)
    gate_weight, gate = front(gate_t, list(first_pieces), None)
    up_weight, up, *hidden = front(up_t, [ROW_CHUNKS + i for i in first_pieces], gate)
    hidden, other_hidden = joined(hidden), joined(swapped(hidden))
    cot_all = joined(cot_parts)

    width = half // n_groups // COL_CHUNKS
    down_weights, layers, sent, prob_part = [], [], [], 0.0
    made = ()
    for part in range(COL_CHUNKS):
        keys, pieces = zip(*y[2 * ROW_CHUNKS + part])
        weight, *made = call(
            functools.partial(out_kernel, sizes, keys, part),
            [shape(2 * wide, n_groups * width, BF16)] + [shape(each, n_groups * width, BF16)] * blocks,
            (hidden, other_hidden, down, *pieces),
            made[:1],
        )
        down_weights.append(weight)
        back = list(made)
        if shifted:
            for lane in ([order[-1]], order[:-1]):
                for i, s in enumerate(lane):
                    held = back[lane[i - 1]] if i else sent[-1][lane[-1]] if sent else None
                    out = back[s] if held is None else call(join_kernel, made_shape(back[s]), (back[s],), (held,))
                    back[s] = travel(out, -1, s)
        else:
            back = [travel(back[0], -1, 0)]
        sent.append(back)
        layer, prob, both = call(
            functools.partial(layer_kernel, *routing, n_groups, part),
            [shape(count, n_groups * width, BF16), shape(expert_ids.shape[1], count, F32), shape(count, rows, BF16)],
            (ids_t, probs_t, cotangent, *back),
        )
        layers.append(layer)
        prob_part = prob_part + prob

    kept, *crossing = call(
        functools.partial(cot_kernel, n_groups),
        [shape(rows, wide, F32)] + [shape(rows // SWAPS, wide, BF16)] * SWAPS,
        (cot_all, *down_weights),
        made[:1],
    )
    received = joined(swapped(crossing))
    kept, *crossing = call(
        grad_kernel,
        [shape(rows, half, F32)] + [shape(rows // SWAPS, half, BF16)] * SWAPS,
        (gate, up, kept, received, gate_weight, up_weight),
        layers[:1],
    )
    received = joined(swapped(crossing))
    slots = call(add_kernel, [shape(each, half, BF16)] * blocks, (kept, received), [sent[-1][s] for s in order[::2] if shifted])
    grad_back = [travel(part, -1, s) for s, part in enumerate(slots)]
    grad_probs = (prob_part + shift(prob_part, "tensor", 1)).T
    grad_tokens, layer_out = call(
        functools.partial(token_kernel, n_groups),
        [shape(count, half, BF16)] * 2,
        (both, *grad_back, *layers),
    )
    return (layer_out, grad_tokens, grad_probs)


def solution(mesh):
    by_token = ("groups", "expert", "dp")
    weight = P("expert", "dp", "tensor")
    in_specs = (P(by_token, "tensor"), P(by_token, "tensor"), P(by_token, None), P(by_token, None)) + (weight,) * 3
    out_specs = (P(by_token, "tensor"), P(by_token, "tensor"), P(by_token, None))
    return jax.shard_map(local, mesh=mesh, in_specs=in_specs, out_specs=out_specs, check_vma=False)
```

```python
import functools

import jax
import jax.numpy as jnp
from jax import lax
from jax.experimental import pallas as pl
from jax.experimental.pallas import tpu as pltpu
from jax.sharding import PartitionSpec as P

F32 = jnp.float32
BF16 = jnp.bfloat16
LAST = (((1,), (1,)), ((), ()))
ROW_CHUNKS = 2
COL_CHUNKS = 2
SWAPS = 4
SHIFTED_UP_TO = 8

VMEM = pl.BlockSpec(memory_space=pltpu.VMEM)
ANY = pl.BlockSpec(memory_space=pl.ANY)


def dot(a, b, dims=(((1,), (0,)), ((), ()))):
    return lax.dot_general(a, b, dims, preferred_element_type=F32)


def call(kernel, out_shape, args, held=(), scratch=()):
    several = isinstance(out_shape, list)
    given = len(args)

    def body(*refs):
        kernel(*refs[:given], *refs[given + len(held) :])

    return pl.pallas_call(
        body,
        out_shape=out_shape,
        in_specs=[VMEM] * given + [ANY] * len(held),
        out_specs=[VMEM] * len(out_shape) if several else VMEM,
        scratch_shapes=list(scratch),
        compiler_params=pltpu.CompilerParams(vmem_limit_bytes=24 * 1024 * 1024),
        cost_estimate=pl.CostEstimate(flops=1, bytes_accessed=1, transcendentals=0),
    )(*args, *held)


def shape(rows, cols, dtype):
    return jax.ShapeDtypeStruct((rows, cols), dtype)


def made_shape(value):
    return shape(*value.shape, value.dtype)


def padded(size):
    return -(-size // 128) * 128


def before(index, step, size):
    moved = index - step
    return jnp.where(moved < 0, moved + size, moved)


def rows_at(start, size):
    return pl.ds(pl.multiple_of(start, 16), size)


def cols_at(start, size):
    return pl.ds(pl.multiple_of(start, 128), size)


def places(experts, cap, rotated, start, size, ids_t):
    count = ids_t.shape[1]
    row = lax.broadcasted_iota(jnp.int32, (size, 1), 0) + start
    block = jnp.zeros_like(row)
    for later in range(1, experts):
        block = block + (row >= later * cap).astype(jnp.int32)
    expert = block + (lax.axis_index("expert") if rotated else 0)
    expert = jnp.where(expert >= experts, expert - experts, expert)
    slot = (row - block * cap).astype(F32)
    first = ids_t[0:1, :] == expert
    second = ids_t[1:2, :] == expert
    before_it = lax.broadcasted_iota(jnp.int32, (count, count), 0) < lax.broadcasted_iota(jnp.int32, (count, count), 1)
    earlier = dot((first | second).astype(F32).astype(BF16), before_it.astype(F32).astype(BF16))
    here = earlier == slot
    return first & here, second & here


def rows_kernel(experts, cap, rotated, blocks, ids_t, probs_t, tok, cot, *outs):
    each = outs[0].shape[0] // 2
    for block, out in zip(blocks, outs):
        first, second = places(experts, cap, rotated, block * each, each, ids_t)
        weight = jnp.where(first, probs_t[0:1, :], jnp.where(second, probs_t[1:2, :], 0.0))
        weight = jnp.sum(weight, axis=1, keepdims=True)
        chosen = (first | second).astype(F32).astype(BF16)
        out[pl.ds(0, each), :] = dot(chosen, tok[...]).astype(BF16)
        out[pl.ds(each, each), :] = (weight * dot(chosen, cot[...])).astype(BF16)


def halve_kernel(both, *outs):
    put_rows(both[...], outs)


def cut_kernel(axis, chunk, n_groups, weight, out):
    size = out.shape[axis]
    start = lax.axis_index("groups") * (weight.shape[axis] // n_groups) + chunk * size
    out[...] = weight[rows_at(start, size), :] if axis == 0 else weight[:, cols_at(start, size)]


def join_kernel(*refs):
    at = 0
    for part in refs[:-1]:
        refs[-1][pl.ds(at, part.shape[0]), :] = part[...]
        at += part.shape[0]


def fill_wide(sizes, own, pieces, dst):
    n_dp, n_groups = sizes
    units, feats = own.shape
    group, place = lax.axis_index("groups"), lax.axis_index("dp")
    dst[pl.ds(0, units), cols_at(place * feats, feats)] = own[...]
    share = units // n_groups
    for (chunk, step, turn), ref in pieces:
        start = before(group, turn, n_groups) * share + chunk * ref.shape[0]
        dst[rows_at(start, ref.shape[0]), cols_at(before(place, step, n_dp) * feats, feats)] = ref[...]
    if dst.shape[0] > units:
        dst[units:, :] = jnp.zeros((dst.shape[0] - units, dst.shape[1]), dst.dtype)


def fill_down(sizes, part, own, pieces, dst):
    n_dp, n_groups = sizes
    units, feats = own.shape
    half = dst.shape[0] // 2
    per_half = n_dp // 2
    share = feats // n_groups
    width = share // COL_CHUNKS
    group, place = lax.axis_index("groups"), lax.axis_index("dp")

    def start(index):
        upper = (index >= per_half).astype(jnp.int32)
        return upper * half + (index - upper * per_half) * units

    for g in range(n_groups):
        dst[rows_at(start(place), units), pl.ds(g * width, width)] = own[:, pl.ds(g * share + part * width, width)]
    for (_, step, turn), ref in pieces:
        cols = cols_at(before(group, turn, n_groups) * width, width)
        dst[rows_at(start(before(place, step, n_dp)), units), cols] = ref[...]
    used = per_half * units
    if half > used:
        for side in range(2):
            dst[side * half + used : (side + 1) * half, :] = jnp.zeros((half - used, dst.shape[1]), dst.dtype)


def put_rows(value, outs):
    each = outs[0].shape[0]
    for i, out in enumerate(outs):
        out[...] = value[i * each : (i + 1) * each].astype(out.dtype)


def halves(size):
    core = lax.axis_index("tensor")
    return core * size, (1 - core) * size


def front_kernel(sizes, keys, final, own_tok, other_tok, own, *refs):
    pieces, refs = list(zip(keys, refs[: len(keys)])), refs[len(keys) :]
    weight, act_out = refs[:2] if not final else refs[1:3]
    fill_wide(sizes, own, pieces, weight)
    half = own_tok.shape[1]
    mine, theirs = halves(half)
    value = dot(own_tok[...], weight[:, cols_at(mine, half)], LAST) + dot(other_tok[...], weight[:, cols_at(theirs, half)], LAST)
    act_out[...] = value
    if final:
        gate, hidden_out = refs[0], refs[3:]
        hidden = (gate[...] * jax.nn.sigmoid(gate[...]) * value).astype(BF16)
        put_rows(hidden, hidden_out)


def out_kernel(sizes, keys, part, own_hidden, other_hidden, own, *refs):
    pieces, (weight, *outs) = list(zip(keys, refs[: len(keys)])), refs[len(keys) :]
    fill_down(sizes, part, own, pieces, weight)
    last_out_kernel(own_hidden, other_hidden, weight, *outs)


def last_out_kernel(own_hidden, other_hidden, weight, *outs):
    half = own_hidden.shape[1]
    mine, theirs = halves(half)
    value = dot(own_hidden[...], weight[rows_at(mine, half), :]) + dot(other_hidden[...], weight[rows_at(theirs, half), :])
    put_rows(value, outs)


def cot_kernel(sizes, keys, cots, own, *refs):
    pieces, refs = list(zip(keys, refs[: len(keys)])), refs[len(keys) :]
    weights, (made, keep), send = refs[: COL_CHUNKS - 1], refs[COL_CHUNKS - 1 : COL_CHUNKS + 1], refs[COL_CHUNKS + 1 :]
    fill_down(sizes, COL_CHUNKS - 1, own, pieces, made)
    weights = [*weights, made]
    half, n_groups = keep.shape[1], sizes[1]
    share = cots.shape[1] // n_groups
    width = share // COL_CHUNKS
    mine, theirs = halves(half)
    for start, outs in ((theirs, send), (mine, [keep])):
        total = 0.0
        for part, weight in enumerate(weights):
            for g in range(n_groups):
                rows = cots[:, pl.ds(g * share + part * width, width)]
                total = total + dot(rows, weight[rows_at(start, half), pl.ds(g * width, width)], LAST)
        put_rows(total, outs)


def grad_kernel(gate, up, kept, received, w_gate, w_up, keep, *send):
    gate_act = gate[...]
    sigmoid_g = jax.nn.sigmoid(gate_act)
    hidden_grad = kept[...] + received[...].astype(F32)
    gate_grad = (hidden_grad * up[...] * sigmoid_g * (1.0 + gate_act * (1.0 - sigmoid_g))).astype(BF16)
    up_grad = (hidden_grad * gate_act * sigmoid_g).astype(BF16)
    half = keep.shape[1]
    mine, theirs = halves(half)
    for start, outs in ((theirs, send), (mine, [keep])):
        cols = cols_at(start, half)
        put_rows(dot(gate_grad, w_gate[:, cols]) + dot(up_grad, w_up[:, cols]), outs)


def add_kernel(kept, received, *outs):
    put_rows(kept[...] + received[...].astype(F32), outs)


def layer_kernel(experts, cap, rotated, n_groups, part, ids_t, probs_t, cot, *refs):
    back, (out, prob_out, both_out) = refs[:-3], refs[-3:]
    share = cot.shape[1] // n_groups
    width = share // COL_CHUNKS
    back = jnp.concatenate([r[...] for r in back], axis=0)
    first, second = (m.astype(F32).T.astype(BF16) for m in places(experts, cap, rotated, 0, back.shape[0], ids_t))
    both_out[...] = first + second
    probs = jnp.concatenate([probs_t[...], jnp.zeros((6, probs_t.shape[1]), F32)], axis=0).T
    slots = dot(first, back), dot(second, back)
    out[...] = (probs[:, 0:1] * slots[0] + probs[:, 1:2] * slots[1]).astype(BF16)
    sums = [0.0, 0.0]
    for g in range(n_groups):
        cot_here = cot[:, pl.ds(g * share + part * width, width)].astype(F32)
        for k in range(2):
            sums[k] = sums[k] + jnp.sum(slots[k][:, g * width : (g + 1) * width] * cot_here, axis=1, keepdims=True)
    lane = lax.broadcasted_iota(jnp.int32, (cot.shape[0], 128), 1)
    prob_out[...] = jnp.where(lane == 0, sums[0], sums[1]).T[0:2, :]


def token_kernel(n_groups, both, *refs):
    back, layers, (grad_out, layer_out) = refs[: -2 - COL_CHUNKS], refs[-2 - COL_CHUNKS : -2], refs[-2:]
    width = layers[0].shape[1] // n_groups
    for part, layer in enumerate(layers):
        for g in range(n_groups):
            layer_out[:, pl.ds((g * COL_CHUNKS + part) * width, width)] = layer[:, pl.ds(g * width, width)]
    grad_out[...] = dot(both[...], jnp.concatenate([r[...] for r in back], axis=0)).astype(BF16)


def shift(value, axis, step):
    size = lax.axis_size(axis)
    return lax.ppermute(value, axis, [(i, (i + step) % size) for i in range(size)])


def swapped(parts):
    return [shift(part, "tensor", 1) for part in parts]


def joined(parts):
    if len(parts) == 1:
        return parts[0]
    return call(join_kernel, shape(sum(p.shape[0] for p in parts), parts[0].shape[1], parts[0].dtype), parts)


def local(tokens, cotangent, expert_ids, gate_probs, w_gate, w_up, w_down):
    count, half = tokens.shape
    experts, n_dp, n_groups = lax.axis_size("expert"), lax.axis_size("dp"), lax.axis_size("groups")
    sizes = (n_dp, n_groups)
    cap = 3 * count * expert_ids.shape[1] // (2 * experts)
    rows = experts * cap
    shifted = experts <= SHIFTED_UP_TO
    blocks = experts if shifted else 1
    each = rows // blocks
    routing = (experts, cap, shifted)
    order = sorted(range(1, experts), key=lambda s: min(s, experts - s))

    def travel(part, sign, s):
        if shifted:
            return shift(part, "expert", sign * s) if s else part
        part = lax.all_to_all(part.reshape(experts, cap, -1), "expert", split_axis=0, concat_axis=0, tiled=True)
        return part.reshape(rows, -1)

    gate_t, up_t, down = jnp.swapaxes(w_gate[0], 0, 1), jnp.swapaxes(w_up[0], 0, 1), w_down[0]
    ids_t, probs_t = expert_ids.T, gate_probs.T
    units = gate_t.shape[0]
    wide = padded(units)
    feats = n_dp * gate_t.shape[1]
    plan = [(gate_t, 0, c) for c in range(ROW_CHUNKS)] + [(up_t, 0, c) for c in range(ROW_CHUNKS)]
    plan += [(down, 1, c) for c in range(COL_CHUNKS)]
    x, y, cuts, turned = {}, {}, [], {}

    def last_y(i):
        return y[i][-1][1]

    def cut(i, *held):
        weight, axis, chunk = plan[i]
        size = weight.shape[axis] // n_groups // (COL_CHUNKS if axis else ROW_CHUNKS)
        mine = call(
            functools.partial(cut_kernel, axis, chunk, n_groups),
            shape(weight.shape[0] if axis else size, size if axis else weight.shape[1], BF16),
            (weight,),
            (*held, *cuts[-1:]),
        )
        cuts.append(mine)
        x[i] = [shift(mine, "dp", step) for step in range(1, n_dp)]

    def turn_over(i, *held):
        y[i] = []
        for step, here in enumerate(x[i], 1):
            on = call(join_kernel, made_shape(here), (here,), held)
            turned[i] = on
            for turn in range(n_groups):
                y[i].append(((plan[i][2], step, turn), shift(on, "groups", turn) if turn else here))

    cut(0)
    cut(1)

    def send(picked, *held):
        made = call(
            functools.partial(rows_kernel, *routing, picked),
            [shape(2 * each, half, BF16)] * len(picked),
            (ids_t, probs_t, tokens, cotangent),
            held,
        )
        return [travel(part, 1, s) if shifted else part for part, s in zip(made, picked)]

    def halved(both):
        return call(halve_kernel, [shape(each, half, BF16)] * 2, (both,))

    blocks_in = {}
    for i in range(len(plan)):
        turn = i // 2
        if shifted and i % 2 == 0 and turn < len(order):
            s = order[turn]
            if turn:
                (blocks_in[s],) = send((s,), blocks_in[order[turn - 1]], turned[i - 2])
            else:
                blocks_in[0], blocks_in[s] = send((0, s), cuts[0])
        turn_over(i, *([last_y(i - 2)] if i > 1 else []))
        if i + 2 < len(plan):
            cut(i + 2, x[i][-1], *([last_y(i - 1)] if i else []))
    for turn in range(len(plan) // 2, len(order) if shifted else 0):
        (blocks_in[order[turn]],) = send((order[turn],), blocks_in[order[turn - 1]])
    if shifted:
        tok_parts, cot_parts = zip(*[halved(blocks_in[s]) for s in range(blocks)])
    else:
        tok_part, cot_part = halved(send((0,))[0])
        tok_parts, cot_parts = [travel(tok_part, 1, 0)], [travel(cot_part, 1, 0)]
    tok_all, other_tok = joined(tok_parts), joined(swapped(tok_parts))

    def front(own, picked, gate):
        final = gate is not None
        keys, pieces = zip(*[kp for i in picked for kp in y[i]])
        act = shape(rows, wide, F32)
        return call(
            functools.partial(front_kernel, sizes, keys, final),
            [shape(wide, feats, BF16), act] + ([shape(rows // SWAPS, wide, BF16)] * SWAPS if final else []),
            (tok_all, other_tok, own, *pieces, *([gate] if final else [])),
        )

    first_pieces = range(ROW_CHUNKS)
    gate_weight, gate = front(gate_t, list(first_pieces), None)
    up_weight, up, *hidden = front(up_t, [ROW_CHUNKS + i for i in first_pieces], gate)
    hidden, other_hidden = joined(hidden), joined(swapped(hidden))
    cot_all = joined(cot_parts)

    width = half // n_groups // COL_CHUNKS

    def outputs(part):
        keys, pieces = zip(*y[2 * ROW_CHUNKS + part])
        weight, *made = call(
            functools.partial(out_kernel, sizes, keys, part),
            [shape(2 * wide, n_groups * width, BF16)] + [shape(each, n_groups * width, BF16)] * blocks,
            (hidden, other_hidden, down, *pieces),
        )
        return weight, [travel(out, -1, s) for s, out in enumerate(made)]

    def layer(part, back):
        return call(
            functools.partial(layer_kernel, *routing, n_groups, part),
            [shape(count, n_groups * width, BF16), shape(expert_ids.shape[1], count, F32), shape(count, rows, BF16)],
            (ids_t, probs_t, cotangent, *back),
        )

    down_weights, sent = [None] * COL_CHUNKS, [None] * COL_CHUNKS
    for part in range(COL_CHUNKS - 1):
        down_weights[part], sent[part] = outputs(part)
    early = [sent[0][s] for s in order] if shifted else []
    weight, kept, *crossing = call(
        functools.partial(cot_kernel, sizes, [key for key, _ in y[len(plan) - 1]]),
        [shape(2 * wide, n_groups * width, BF16), shape(rows, wide, F32)] + [shape(rows // SWAPS, wide, BF16)] * SWAPS,
        (cot_all, down, *[piece for _, piece in y[len(plan) - 1]], *down_weights[:-1]),
        early[:2],
    )
    down_weights[-1] = weight
    last_made = call(
        last_out_kernel,
        [shape(each, n_groups * width, BF16)] * blocks,
        (hidden, other_hidden, weight),
        [kept, *early[2:]],
    )
    sent[-1] = [travel(out, -1, s) for s, out in enumerate(last_made)]
    received = joined(swapped(crossing))
    kept, *crossing = call(
        grad_kernel,
        [shape(rows, half, F32)] + [shape(rows // SWAPS, half, BF16)] * SWAPS,
        (gate, up, kept, received, gate_weight, up_weight),
        early,
    )
    received = joined(swapped(crossing))
    slots = call(add_kernel, [shape(each, half, BF16)] * blocks, (kept, received), [sent[-1][s] for s in order[::2] if shifted])
    grad_back = [travel(part, -1, s) for s, part in enumerate(slots)]
    layers = [layer(part, back) for part, back in enumerate(sent)]
    prob_part = sum(prob for _, prob, _ in layers)
    both = layers[0][2]
    layers = [out for out, _, _ in layers]
    grad_probs = (prob_part + shift(prob_part, "tensor", 1)).T
    grad_tokens, layer_out = call(
        functools.partial(token_kernel, n_groups),
        [shape(count, half, BF16)] * 2,
        (both, *grad_back, *layers),
    )
    return (layer_out, grad_tokens, grad_probs)


def solution(mesh):
    by_token = ("groups", "expert", "dp")
    weight = P("expert", "dp", "tensor")
    in_specs = (P(by_token, "tensor"), P(by_token, "tensor"), P(by_token, None), P(by_token, None)) + (weight,) * 3
    out_specs = (P(by_token, "tensor"), P(by_token, "tensor"), P(by_token, None))
    return jax.shard_map(local, mesh=mesh, in_specs=in_specs, out_specs=out_specs, check_vma=False)
```
